32 devices in a mesh: ctx: 16 (over z, y, x), wt: 2 (over core).
Axes of the slice: x: 2, y: 2, z: 4, core: 2. Of those that a mesh axis runs over, the one named last changes fastest.
Arguments:
- tokens: bfloat16 [2, 2048, 2048], P('wt', 'ctx'), may hold values from -6 to 6
- gain_attn: bfloat16 [2048], P('wt'), may hold values from 0.5 to 1.5
- w_query: bfloat16 [2048, 3072], P('wt'), may hold values from -0.125 to 0.125
- w_kv_down: bfloat16 [2048, 576], P('wt'), may hold values from -0.125 to 0.125
- gain_kv: bfloat16 [512], P('wt'), may hold values from 0.5 to 1.5
- w_kv_up: bfloat16 [512, 4096], P('wt'), may hold values from -0.25 to 0.25
- w_out: bfloat16 [2048, 2048], P('wt'), may hold values from -1 to 1
- gain_mlp: bfloat16 [2048], P('wt'), may hold values from 0.5 to 1.5
- w_shared_gate: bfloat16 [2048, 2816], P('wt'), may hold values from -0.125 to 0.125
- w_shared_up: bfloat16 [2048, 2816], P('wt'), may hold values from -0.125 to 0.125
- w_shared_down: bfloat16 [2816, 2048], P('wt'), may hold values from -0.109375 to 0.109375
- w_expert_gate: bfloat16 [16, 2048, 1408], P('ctx', 'wt'), may hold values from -0.125 to 0.125
- w_expert_up: bfloat16 [16, 2048, 1408], P('ctx', 'wt'), may hold values from -0.125 to 0.125
- w_expert_down: bfloat16 [16, 1408, 2048], P('ctx', 'wt'), may hold values from -0.21875 to 0.21875
- block_deal: int32 [32], replicated, may hold values from 0 to 31, as said below
- lengths: int32 [2, 4], P('wt'), may hold values from 1 to 1536, 2048 in all within a row
- routes: int32 [2, 2048, 6], P('wt', 'ctx'), may hold values from 0 to 15, all different within a row; in each aligned block of 128 rows (0 to 127, 128 to 255, ..., all dimensions but the last counted through in order) at most 64 rows name the same one
- gate_weights: float32 [2, 2048, 6], P('wt', 'ctx'), may hold values from 0.16 to 0.64
- cotangent: bfloat16 [2, 2048, 2048], P('wt', 'ctx'), may hold values from -6 to 6
Outputs:
- mixed_out: bfloat16 [2, 2048, 2048], P('wt', 'ctx')
- grad_tokens: float32 [2, 2048, 2048], P('wt', 'ctx')
- grad_gain_attn: float32 [2048], P(('ctx', 'wt'))
- grad_w_query: float32 [2048, 3072], P(None, ('ctx', 'wt'))
- grad_w_kv_down: float32 [2048, 576], P(('ctx', 'wt'))
- grad_gain_kv: float32 [512], P(('ctx', 'wt'))
- grad_w_kv_up: float32 [512, 4096], P(None, ('ctx', 'wt'))
- grad_w_out: float32 [2048, 2048], P(None, ('ctx', 'wt'))
- grad_gain_mlp: float32 [2048], P(('ctx', 'wt'))
- grad_w_shared_gate: float32 [2048, 2816], P(('ctx', 'wt'))
- grad_w_shared_up: float32 [2048, 2816], P(('ctx', 'wt'))
- grad_w_shared_down: float32 [2816, 2048], P(None, ('ctx', 'wt'))
- grad_w_expert_gate: float32 [16, 2048, 1408], P('ctx', 'wt')
- grad_w_expert_up: float32 [16, 2048, 1408], P('ctx', 'wt')
- grad_w_expert_down: float32 [16, 1408, 2048], P('ctx', 'wt')
The draws below stay inside these ranges and needn't reach their ends.
Inputs may be any that keep to these rules, and one draw needn't show every extreme that they name: Index i of ctx holds the group's blocks block_deal[2i] and block_deal[2i+1], which sum to 31; every block is dealt once. `lengths`: each row sums to 2048, and its largest entry is exactly 1536. `routes`: A token names 6 different experts. In the rows of one device no expert is named by more than 64 rows, a bound that some block reaches.
All inputs are finite; a program needn't handle non-finite values.
Results may differ from the reference program's by a relative error of at most 0.02.
Values may be sent and summed in bfloat16 or wider, within the bound.
No kernel may reach another device: no remote copies, remote signals or barrier semaphores. Data moves between devices by JAX's collectives and lax.ppermute only.
A program may use at most 384 MiB of HBM per device.

```python
import math
import jax
import jax.numpy as jnp
import numpy as np
from jax import lax

D = 2048
H = 16
DN = 128
DR = 64
DV = 128
R = 512
FE = 1408
TOP = 6
TOK_DEV = 128
SEQS = 4
FS = 2816
GROUP = 2048
BLK = 64
LONGEST = 1536
EXPERTS = 16
CAP = 64
N_CTX = 16
N_WT = 2


def draw_block_deal(key, part):
    key = jax.random.fold_in(key, 7)
    order = jax.random.permutation(key, N_CTX).astype(jnp.int32)
    mirror = 2 * N_CTX - 1 - order
    return jnp.stack([order, mirror], axis=1).reshape(2 * N_CTX).astype(jnp.int32)


def steps_of(stream_key, shape, shards, smallest, largest):
    gain, own = 1.0, jax.random.fold_in(stream_key, 6)
    for dim, shards_of in shards:
        steps = jnp.exp(jax.random.uniform(jax.random.fold_in(own, dim), (shards_of,), jnp.float32, smallest / len(shards), largest / len(shards)))
        gain = gain * jnp.repeat(steps, shape[dim] // shards_of).reshape([-1 if axis == dim else 1 for axis in range(len(shape))])
    return gain


def split_up(number_of, total, reach, lean):
    loads = [(1 << 20) // math.isqrt(rank ** lean) + 1 for rank in range(2, number_of + 1)]
    spare, counts = total - reach - (number_of - 1), [1] * (number_of - 1)
    while spare > 0:
        movable = [i for i in range(number_of - 1) if counts[i] < reach]
        pool, left = sum([loads[i] for i in movable]), spare
        for i in movable:
            extra = min(reach - counts[i], max(1, left * loads[i] // pool), spare)
            counts[i] = counts[i] + extra
            spare = spare - extra
    return np.array([reach] + counts)


def uneven_parts(own_key, count, total, reach, slope):
    if count == 2:
        one = jax.random.randint(own_key, (), max(1, total - reach), min(reach, total - 1) + 1)
        return jnp.stack([one, total - one])
    sizes = jnp.asarray(split_up(count, total, reach, slope), jnp.int32)
    couples = (count - 1) // 2
    source_of, sink = sizes[1:1 + 2 * couples:2], sizes[2:2 + 2 * couples:2]
    room = jnp.minimum(source_of - 1, reach - sink)
    moved = jax.random.randint(jax.random.fold_in(own_key, 1), (couples,), 0, 1 << 20) % (room + 1)
    sizes = sizes.at[1:1 + 2 * couples:2].set(source_of - moved).at[2:2 + 2 * couples:2].set(sink + moved)
    return sizes[jax.random.permutation(jax.random.fold_in(own_key, 2), count)]


def routed_block(key, own, number, rows, count, top, most, skew):
    sequence = jax.random.permutation(key, count)
    packed, usual = portions_of(count, rows * top, most, skew, True), portions_of(count, rows * top, most, skew, False)
    places = jnp.arange(count)

    def named(sizes, rotation):
        used = int((sizes > 0).sum())
        fixed = max(1, used // 4)
        passed = fixed + (places - fixed + rotation * (used - fixed)) % max(1, count - fixed)
        return jnp.zeros((count,), jnp.int32).at[sequence[jnp.where(places < fixed, places, passed)]].set(jnp.asarray(sizes, jnp.int32))

    sizes = jnp.where(number % 4 == 0, named(packed, number // 4), named(usual, number - number // 4 - 1))
    mixed = jax.random.permutation(jax.random.fold_in(own, 3), count)
    source_of, sink = mixed[0:count // 2 * 2:2], mixed[1:count // 2 * 2:2]
    room = jnp.minimum(sizes[source_of] - 1, most - sizes[sink]) // 2
    room = jnp.where((source_of == sequence[0]) | (sink == sequence[0]) | (sizes[sink] == 0), 0, jnp.maximum(room, 0))
    passed = jax.random.randint(jax.random.fold_in(own, 4), (count // 2,), 0, 1 << 20) % (room + 1)
    sizes = sizes.at[source_of].add(-passed).at[sink].add(passed)
    items = jnp.searchsorted(jnp.cumsum(sizes), jnp.arange(rows * top), side="right").astype(jnp.int32)
    table = items.reshape(top, rows).T
    table = table[jax.random.permutation(jax.random.fold_in(own, 1), rows)]
    rotation = jax.random.randint(jax.random.fold_in(own, 2), (rows, 1), 0, top)
    return jnp.take_along_axis(table, (jnp.arange(top)[None, :] + rotation) % top, axis=1)


def portions_of(number_of, total, bound, lean, full):
    loads = [(1 << 20) // math.isqrt(standing ** lean) + 1 for standing in range(1, number_of + 1)]
    largest = bound if full else min(bound, max(-(-total // number_of), total * loads[0] // sum(loads)))
    least = 1 if total - largest >= number_of - 1 else 0
    holding, rest = [largest] + [least] * (number_of - 1), total - largest - least * (number_of - 1)
    while rest > 0:
        free = [i for i in range(1, number_of) if holding[i] < largest] or [i for i in range(1, number_of) if holding[i] < bound]
        whole, remaining = sum([loads[i] for i in free]), rest
        for i in free:
            extra = min(bound - holding[i], max(1, remaining * loads[i] // whole), rest)
            holding[i] = holding[i] + extra
            rest = rest - extra
    return np.array(holding)


def gaussian(stream_key, shape, width, most, split=(), kind=jnp.bfloat16):
    factor_of = steps_of(stream_key, shape, split, -0.22, 0.18) if split else 1.0
    array = jax.random.normal(stream_key, shape, jnp.float32) * width * factor_of
    return jnp.minimum(jnp.maximum(array, -most), most).astype(kind)


def setup_inputs(seed: int = 0) -> dict:
    splits = jax.random.split(jax.random.key(seed), 20)
    tokens = gaussian(splits[0], (N_WT, GROUP, D), 1.0, 6.0, ((0, 2), (1, 16)))
    gain_attn = jnp.clip(1.0 + 0.1 * jax.random.normal(splits[1], (D,), jnp.float32), 0.5, 1.5).astype(jnp.bfloat16)
    w_query = gaussian(splits[2], (D, H * (DN + DR)), D ** -0.5, 0.125, ((0, 2),))
    w_kv_down = gaussian(splits[3], (D, R + DR), D ** -0.5, 0.125, ((0, 2),))
    gain_kv = jnp.clip(1.0 + 0.1 * jax.random.normal(splits[4], (R,), jnp.float32), 0.5, 1.5).astype(jnp.bfloat16)
    w_kv_up = gaussian(splits[5], (R, H * (DN + DV)), R ** -0.5, 0.25, ((0, 2),))
    w_out = gaussian(splits[6], (H * DV, D), (max(1, H * DV // 64)) ** -0.5, 1.0, ((0, 2),))
    gain_mlp = jnp.clip(1.0 + 0.1 * jax.random.normal(splits[7], (D,), jnp.float32), 0.5, 1.5).astype(jnp.bfloat16)
    w_shared_gate = gaussian(splits[8], (D, FS), D ** -0.5, 0.125, ((0, 2),))
    w_shared_up = gaussian(splits[9], (D, FS), D ** -0.5, 0.125, ((0, 2),))
    w_shared_down = gaussian(splits[10], (FS, D), FS ** -0.5, 0.109375, ((0, 2),))
    w_expert_gate = gaussian(splits[11], (EXPERTS, D, FE), D ** -0.5, 0.125, ((0, 16), (1, 2)))
    w_expert_up = gaussian(splits[12], (EXPERTS, D, FE), D ** -0.5, 0.125, ((0, 16), (1, 2)))
    w_expert_down = gaussian(splits[13], (EXPERTS, FE, D), (max(1, FE // 2)) ** -0.5, 0.21875, ((0, 16), (1, 2)))
    block_deal = draw_block_deal(jax.random.fold_in(splits[19], 71), 0)
    lengths = jax.vmap(lambda own: uneven_parts(own, SEQS, GROUP, LONGEST, 2))(jax.random.split(splits[15], N_WT)).reshape((N_WT, SEQS)).astype(jnp.int32)
    routes_keys = jax.random.split(jax.random.fold_in(splits[16], 1), N_WT * GROUP // TOK_DEV)
    routes_turns = jax.random.permutation(jax.random.fold_in(splits[16], 3), N_WT * GROUP // TOK_DEV)
    routes = jax.vmap(lambda own, number: routed_block(jax.random.fold_in(splits[16], 2), own, number, TOK_DEV, EXPERTS, TOP, CAP, 2))(routes_keys, routes_turns).reshape((N_WT, GROUP, TOP))
    gate_weights = jnp.clip(jnp.exp(math.log(0.64) - 1.3862944 * jax.random.uniform(splits[17], (N_WT, GROUP, TOP), jnp.float32) ** steps_of(splits[17], (N_WT, GROUP, TOP), ((0, 2), (1, 16)), -0.2, 0.2)), 0.16, 0.64)
    cotangent = gaussian(splits[18], (N_WT, GROUP, D), 1.0, 6.0, ((0, 2), (1, 16)))
    return {"tokens": tokens, "gain_attn": gain_attn, "w_query": w_query, "w_kv_down": w_kv_down, "gain_kv": gain_kv, "w_kv_up": w_kv_up, "w_out": w_out, "gain_mlp": gain_mlp, "w_shared_gate": w_shared_gate, "w_shared_up": w_shared_up, "w_shared_down": w_shared_down, "w_expert_gate": w_expert_gate, "w_expert_up": w_expert_up, "w_expert_down": w_expert_down, "block_deal": block_deal, "lengths": lengths, "routes": routes, "gate_weights": gate_weights, "cotangent": cotangent}


@jax.custom_vjp
def low(v):
    return lax.optimization_barrier(v.astype(jnp.bfloat16)).astype(jnp.float32)

@jax.custom_vjp
def low_back(v):
    return v

def low_keep(v):
    return (low(v), None)

def low_pass(kept, grad):
    return (grad,)

def back_keep(v):
    return (v, None)

def back_low(kept, grad):
    return (low(grad),)
low.defvjp(low_keep, low_pass)
low_back.defvjp(back_keep, back_low)
EPS = 1e-06
HIGHEST = lax.Precision.HIGHEST

def both_ways(values):
    return low_back(low(values))

def rms_norm(values, gain_in, reduce_axis):
    return values * lax.rsqrt(lax.optimization_barrier(jnp.mean(values * values, axis=reduce_axis, keepdims=True)) + EPS) * gain_in

def rope_angles(position, rope_width):
    half_width = rope_width // 2
    frequency = jnp.exp(jnp.arange(half_width, dtype=jnp.float32) * (-2.0 * math.log(10000.0) / rope_width))
    angles = position.astype(jnp.float32)[:, None] * frequency[None, :]
    return (jnp.cos(angles), jnp.sin(angles))

def rotate(values, cos_table, sin_table, rope_axis):
    half_width = values.shape[rope_axis] // 2
    first_half = lax.slice_in_dim(values, 0, half_width, axis=rope_axis)
    second_half = lax.slice_in_dim(values, half_width, 2 * half_width, axis=rope_axis)
    return jnp.concatenate([first_half * cos_table - second_half * sin_table, first_half * sin_table + second_half * cos_table], axis=rope_axis)

def token_layout(block_deal, lengths_row, first_row, row_count, block_rows):
    row_ids = first_row + jnp.arange(row_count, dtype=jnp.int32)
    blocks = row_ids // block_rows
    block_ids = jnp.arange(block_deal.shape[0], dtype=jnp.int32)
    picked = lax.optimization_barrier(jnp.sum(jnp.where(blocks[:, None] == block_ids[None, :], block_deal[None, :], 0), axis=1)).astype(jnp.int32)
    place_at = picked * block_rows + row_ids % block_rows
    seq_ends = jnp.cumsum(lengths_row).astype(jnp.int32)
    past_end = place_at[:, None] >= seq_ends[None, :]
    segment = lax.optimization_barrier(jnp.sum(past_end.astype(jnp.int32), axis=1)).astype(jnp.int32)
    seq_start = lax.optimization_barrier(jnp.sum(jnp.where(past_end, lengths_row[None, :], 0), axis=1)).astype(jnp.int32)
    return (place_at, segment, place_at - seq_start)

def attend_block(query_latent, query_rope, place_q, segment_q, latent, key_rope, place_k, segment_k):
    raw_scores = jnp.einsum('thr,kr->thk', query_latent, latent, precision=HIGHEST) + jnp.einsum('thd,kd->thk', query_rope, key_rope, precision=HIGHEST)
    scores = low_back(raw_scores * (1.0 / math.sqrt(DN + DR)))
    visible = ((segment_k[None, :] == segment_q[:, None]) & (place_k[None, :] <= place_q[:, None]))[:, None, :]
    masked = jnp.where(visible, scores, -1e+30)
    top_score = lax.optimization_barrier(jnp.max(masked, axis=2, keepdims=True))
    weights = jnp.where(visible, jnp.exp(masked - top_score), 0.0)
    probs = low(weights / lax.optimization_barrier(jnp.sum(weights, axis=2, keepdims=True)))
    return jnp.einsum('thk,kr->thr', probs, latent, precision=HIGHEST)

def attend_group(grouped):
    query_latent, query_rope, latent, key_rope, place_at, segment = grouped
    block_size = min(512, GROUP)
    block_count = GROUP // block_size
    pieces = (query_latent.reshape(block_count, block_size, H, R), query_rope.reshape(block_count, block_size, H, DR), place_at.reshape(block_count, block_size), segment.reshape(block_count, block_size))
    checked = jax.checkpoint(attend_block)

    def attend_piece(piece_tuple):
        return checked(piece_tuple[0], piece_tuple[1], piece_tuple[2], piece_tuple[3], latent, key_rope, place_at, segment)
    return lax.map(attend_piece, pieces).reshape(GROUP, H, R)

def expert_apply(normed_two, gate_matrix, up_matrix, down_matrix):
    entering = low_back(normed_two)
    gate_pre = low_back(jnp.dot(entering, gate_matrix, precision=HIGHEST))
    up_pre = low_back(jnp.dot(entering, up_matrix, precision=HIGHEST))
    hidden = low(jax.nn.silu(gate_pre) * up_pre)
    return both_ways(jnp.dot(hidden, down_matrix, precision=HIGHEST))

def forward(float_args, tables):
    inputs, gain_attn, w_query, w_kv_down, gain_kv, w_kv_up, w_out, gain_mlp, w_shared_gate, w_shared_up, w_shared_down, w_expert_gate, w_expert_up, w_expert_down = float_args
    place_at, segment, position, mixing = tables
    row_total = N_WT * GROUP
    flat = inputs.reshape(row_total, D)
    cos_table, sin_table = rope_angles(position.reshape(row_total), DR)
    normed_one = low(rms_norm(flat, gain_attn, -1))
    query_all = low_back(jnp.dot(normed_one, w_query, precision=HIGHEST)).reshape(row_total, H, DN + DR)
    query_nope = low(query_all[:, :, :DN])
    query_rope = low(rotate(query_all[:, :, DN:], cos_table[:, None, :], sin_table[:, None, :], 2))
    kv_up = w_kv_up.reshape(R, H, DN + DV)
    query_latent = both_ways(jnp.einsum('thd,rhd->thr', query_nope, kv_up[:, :, :DN], precision=HIGHEST))
    kv_down = low_back(jnp.dot(normed_one, w_kv_down, precision=HIGHEST))
    latent = low(rms_norm(kv_down[:, :R], gain_kv, -1))
    key_rope = low(rotate(kv_down[:, R:], cos_table, sin_table, 1))
    grouped = (query_latent.reshape(N_WT, GROUP, H, R), query_rope.reshape(N_WT, GROUP, H, DR), latent.reshape(N_WT, GROUP, R), key_rope.reshape(N_WT, GROUP, DR), place_at, segment)
    out_latent = both_ways(lax.map(attend_group, grouped).reshape(row_total, H, R))
    heads_out = both_ways(jnp.einsum('thr,rhv->thv', out_latent, kv_up[:, :, DN:], precision=HIGHEST).reshape(row_total, H * DV))
    residual = flat + low_back(jnp.dot(heads_out, w_out, precision=HIGHEST))
    normed_two = low(rms_norm(residual, gain_mlp, -1))
    shared_gate = low_back(jnp.dot(normed_two, w_shared_gate, precision=HIGHEST))
    shared_up = low_back(jnp.dot(normed_two, w_shared_up, precision=HIGHEST))
    shared_hidden = low(jax.nn.silu(shared_gate) * shared_up)
    shared_out = low_back(jnp.dot(shared_hidden, w_shared_down, precision=HIGHEST))
    checked_expert = jax.checkpoint(expert_apply)

    def expert_step(running, expert_items):
        gate_matrix, up_matrix, down_matrix, column = expert_items
        return (running + column[:, None] * checked_expert(normed_two, gate_matrix, up_matrix, down_matrix), None)
    routed = lax.scan(expert_step, jnp.zeros((row_total, D), jnp.float32), (w_expert_gate, w_expert_up, w_expert_down, mixing.T))[0]
    return (residual + shared_out + routed).reshape(N_WT, GROUP, D)

def reference(tokens, gain_attn, w_query, w_kv_down, gain_kv, w_kv_up, w_out, gain_mlp, w_shared_gate, w_shared_up, w_shared_down, w_expert_gate, w_expert_up, w_expert_down, block_deal, lengths, routes, gate_weights, cotangent):
    layouts = jax.vmap(lambda lengths_row: token_layout(block_deal, lengths_row, 0, GROUP, BLK))(lengths)
    row_total = N_WT * GROUP
    expert_ids = jnp.arange(EXPERTS, dtype=jnp.int32)
    chosen = routes.reshape(row_total, TOP)[:, :, None] == expert_ids[None, None, :]
    mixing = lax.optimization_barrier(jnp.sum(jnp.where(chosen, gate_weights.reshape(row_total, TOP)[:, :, None], 0.0), axis=1))
    tables = (layouts[0], layouts[1], layouts[2], mixing)
    float_args = (tokens.astype(jnp.float32), gain_attn.astype(jnp.float32), w_query.astype(jnp.float32), w_kv_down.astype(jnp.float32), gain_kv.astype(jnp.float32), w_kv_up.astype(jnp.float32), w_out.astype(jnp.float32), gain_mlp.astype(jnp.float32), w_shared_gate.astype(jnp.float32), w_shared_up.astype(jnp.float32), w_shared_down.astype(jnp.float32), w_expert_gate.astype(jnp.float32), w_expert_up.astype(jnp.float32), w_expert_down.astype(jnp.float32))
    primal_out, pull_back = jax.vjp(lambda inputs_tuple: forward(inputs_tuple, tables), float_args)
    grads = pull_back(cotangent.astype(jnp.float32))[0]
    return (primal_out.astype(jnp.bfloat16), grads[0], grads[1], grads[2], grads[3], grads[4], grads[5], grads[6], grads[7], grads[8], grads[9], grads[10], grads[11], grads[12], grads[13])
```

```python
import functools
import math

import jax
import jax.numpy as jnp
from jax import lax
from jax.sharding import PartitionSpec as P

D = 2048
H = 16
DN = 128
DR = 64
DV = 128
R = 512
TOP = 6
DQ = DN + DR
KW = R + DR

EPS = 1e-06
SCALE = 1.0 / math.sqrt(DN + DR)
MASKED = -1e30
BF = jnp.bfloat16
F32 = jnp.float32


def contract(former, latter, former_dim, latter_dim):
    return lax.dot_general(
        former,
        latter,
        (((former_dim,), (latter_dim,)), ((), ())),
        preferred_element_type=F32,
    )


def wt_from(x, step):
    count = lax.axis_size("wt")
    return lax.ppermute(x, "wt", [((i + step) % count, i) for i in range(count)])


def wt_to(x, step):
    count = lax.axis_size("wt")
    return lax.ppermute(x, "wt", [(i, (i + step) % count) for i in range(count)])


def wt_rows(x):
    return jnp.concatenate(
        [x] + [wt_from(x, step) for step in range(1, lax.axis_size("wt"))], axis=0
    )


def in_order(parts, axis):
    count = len(parts)
    w = lax.axis_index("wt")
    if count == 2:
        return jnp.where(
            w == 0, jnp.concatenate(parts, axis), jnp.concatenate(parts[::-1], axis)
        )
    size = parts[0].shape[axis]
    return lax.dynamic_slice_in_dim(
        jnp.concatenate(parts + parts, axis), (count - w) % count * size, count * size, axis
    )


def wt_gather(x, axis):
    return in_order([x] + [wt_from(x, step) for step in range(1, lax.axis_size("wt"))], axis)


def part_of(x, index, axis):
    count = lax.axis_size("wt")
    size = x.shape[axis] // count
    if count == 2:
        return jnp.where(
            index == 0,
            lax.slice_in_dim(x, 0, size, axis=axis),
            lax.slice_in_dim(x, size, 2 * size, axis=axis),
        )
    return lax.dynamic_slice_in_dim(x, index * size, size, axis)


def my_part(x, axis):
    return part_of(x, lax.axis_index("wt"), axis)


def wt_sum_rows(x):
    count = lax.axis_size("wt")
    rows = x.shape[0] // count
    total = x[:rows]
    for step in range(1, count):
        total = total + wt_to(x[step * rows : (step + 1) * rows], step)
    return total


def wt_sum_part(x, axis):
    count = lax.axis_size("wt")
    w = lax.axis_index("wt")
    rows = x.shape[0] // count
    total = my_part(x, axis)
    for step in range(1, count):
        other = wt_to(part_of(x, (w + step) % count, axis), step)
        other = jnp.concatenate([other[step * rows :], other[: step * rows]], axis=0)
        total = total + other
    return total


def wt_own_rows(x):
    count = lax.axis_size("wt")
    rows = x.shape[0] // count
    parts = [x[:rows]]
    for step in range(1, count):
        back = count - step
        parts.append(
            lax.ppermute(
                x[back * rows : (back + 1) * rows],
                "wt",
                [((i + step) % count, i) for i in range(count)],
            )
        )
    return in_order(parts, 1)


def wt_all_columns(x):
    count = lax.axis_size("wt")
    rows = x.shape[0] // count
    parts = [x]
    for step in range(1, count):
        other = wt_from(x, step)
        parts.append(jnp.concatenate([other[-step * rows :], other[: -step * rows]], axis=0))
    return in_order(parts, 1)


def ctx_swap(x, mask):
    count = lax.axis_size("ctx")
    return lax.ppermute(x, "ctx", [(i, i ^ mask) for i in range(count)])


def spread_orders():
    bits = []
    bit = lax.axis_size("ctx") // 2
    while bit:
        bits.append(bit)
        bit //= 2
    return bits, bits[:-2] + [bits[-1], bits[-2]]


def masks_of(order):
    masks = [0]
    for bit in order:
        masks = masks + [m ^ bit for m in masks]
    return masks


def ctx_spread(x, order):
    for bit in order:
        x = jnp.concatenate([x, ctx_swap(x, bit)], axis=0)
    return x


def ctx_unspread(x, order):
    for bit in reversed(order):
        half = x.shape[0] // 2
        x = x[:half] + ctx_swap(x[half:].astype(BF), bit).astype(F32)
    return x


def ctx_reduce(x, order, sent=BF):
    c = lax.axis_index("ctx")
    count = x.shape[0]
    tail = x.shape[1:]
    dims = []
    bit = count // 2
    while bit:
        dims.append(bit)
        bit //= 2
    for number, bit in enumerate(order):
        place = dims.index(bit)
        before, after = 2**place, 2 ** (len(dims) - place - 1)
        view = x.reshape((before, 2, after) + tail)
        mine = (c // bit) % 2
        keep = lax.dynamic_index_in_dim(view, mine, 1, keepdims=False)
        send = lax.dynamic_index_in_dim(view, 1 - mine, 1, keepdims=False)
        got = ctx_swap(send, bit)
        total = keep.astype(F32) + got.astype(F32)
        dims.pop(place)
        x = total.reshape((before * after,) + tail)
        if number < len(order) - 1:
            x = x.astype(sent)
    return x.reshape(tail)


def query_parts(q, cos, sin, up_key):
    rows = q.shape[0]
    q = q.reshape(rows, H, DQ)
    nope = q[:, :, :DN].astype(BF)
    first, second = q[:, :, DN : DN + DR // 2], q[:, :, DN + DR // 2 :]
    cos, sin = cos[:, None], sin[:, None]
    latent = jnp.einsum("thd,rhd->htr", nope, up_key, preferred_element_type=F32).astype(BF)
    rotary = jnp.concatenate([first * cos - second * sin, first * sin + second * cos], axis=2)
    return nope, jnp.concatenate([latent, rotary.astype(BF).transpose(1, 0, 2)], axis=2)


def attend(query, keys, seen, up_value):
    scores = jnp.einsum("htr,kr->htk", query, keys, preferred_element_type=F32) * SCALE
    scores = jnp.where(seen, scores, MASKED)
    top = jnp.max(scores, axis=2, keepdims=True)
    probs = jnp.exp(scores - top)
    total = jnp.sum(probs, axis=2, keepdims=True)
    out = jnp.einsum("htk,kr->htr", probs.astype(BF), keys[:, :R], preferred_element_type=F32) / total
    heads = jnp.einsum("htr,rhv->thv", out.astype(BF), up_value, preferred_element_type=F32)
    return out, top + jnp.log(total), heads.reshape(heads.shape[0], H * DV).astype(BF)


def attend_back(query, keys, seen, up_key, up_value, out, log_total, grad_heads, cos, sin):
    rows = query.shape[1]
    scores = jnp.einsum("htr,kr->htk", query, keys, preferred_element_type=F32) * SCALE
    probs = jnp.exp(jnp.where(seen, scores, MASKED) - log_total)
    grad_out = jnp.einsum(
        "thv,rhv->htr", grad_heads.reshape(rows, H, DV), up_value, preferred_element_type=F32
    ).astype(BF)
    delta = jnp.sum(grad_out.astype(F32) * out, axis=2, keepdims=True)
    grad_probs = jnp.einsum("htr,kr->htk", grad_out, keys[:, :R], preferred_element_type=F32)
    grad_scores = (probs * (grad_probs - delta) * SCALE).astype(BF)
    grad_query = jnp.einsum("htk,kr->htr", grad_scores, keys, preferred_element_type=F32)
    grad_keys = jnp.einsum("htk,htr->kr", grad_scores, query, preferred_element_type=F32)
    values_part = jnp.einsum("htk,htr->kr", probs.astype(BF), grad_out, preferred_element_type=F32)
    grad_keys = grad_keys + jnp.pad(values_part, ((0, 0), (0, DR)))
    grad_latent = grad_query[:, :, :R].astype(BF)
    nope = jnp.einsum("htr,rhd->thd", grad_latent, up_key, preferred_element_type=F32)
    first, second = grad_query[:, :, R : R + DR // 2], grad_query[:, :, R + DR // 2 :]
    rotary = jnp.concatenate([first * cos + second * sin, second * cos - first * sin], axis=2)
    grad_q = jnp.concatenate([nope, rotary.transpose(1, 0, 2)], axis=2).reshape(rows, H * DQ)
    return grad_q.astype(BF), grad_latent, grad_keys


def rms_norm(values, gain):
    scale = lax.rsqrt(jnp.mean(values * values, axis=1, keepdims=True) + EPS)
    return values * scale * gain


def rms_back(values, gain, grad):
    scale = lax.rsqrt(jnp.mean(values * values, axis=1, keepdims=True) + EPS)
    scaled = grad * gain
    inner = jnp.mean(values * scaled, axis=1, keepdims=True)
    return scale * scaled - values * (scale * scale * scale * inner), jnp.sum(grad * values * scale, axis=0)


def silu_parts(v):
    sig = jax.nn.sigmoid(v)
    return v * sig, sig * (1.0 + v * (1.0 - sig))


def token_places(block_deal, lengths_row, first_block, rows, block):
    blocks = lax.dynamic_slice_in_dim(block_deal, first_block, 2, 0)
    place = (blocks[:, None] * block + jnp.arange(block, dtype=jnp.int32)[None, :]).reshape(rows)
    ends = jnp.cumsum(lengths_row)
    past = place[:, None] >= ends[None, :]
    start = jnp.sum(jnp.where(past, lengths_row[None, :], 0), axis=1)
    return place, start


def route_matrices(routes, gates, capacity):
    count = lax.axis_size("ctx")
    rows = routes.shape[0]
    experts = lax.axis_index("ctx") ^ jnp.arange(count // 2, dtype=jnp.int32)
    named = routes[:, :, None] == experts[None, None, :]
    chosen = jnp.any(named, axis=1)
    weight = jnp.sum(jnp.where(named, gates[:, :, None], 0.0), axis=1).T
    earlier = (jnp.arange(rows)[:, None] > jnp.arange(rows)[None, :]).astype(BF)
    rank = contract(chosen.astype(BF), earlier, 0, 1).astype(jnp.int32)
    slots = jnp.arange(capacity, dtype=jnp.int32)
    held = (rank[:, None, :] == slots[None, :, None]) & chosen.T[:, None, :]
    place = held.astype(BF).reshape(-1, rows)
    weighted = jnp.where(held, weight[:, None, :], 0.0).reshape(-1, rows)
    high = weighted.astype(BF)
    low = (weighted - high.astype(F32)).astype(BF)
    return place, high, low


def per_device(
    tokens,
    gain_attn,
    w_query,
    w_kv_down,
    gain_kv,
    w_kv_up,
    w_out,
    gain_mlp,
    w_shared_gate,
    w_shared_up,
    w_shared_down,
    w_expert_gate,
    w_expert_up,
    w_expert_down,
    block_deal,
    lengths,
    routes,
    gate_weights,
    cotangent,
):
    n_ctx = lax.axis_size("ctx")
    n_wt = lax.axis_size("wt")
    c = lax.axis_index("ctx")
    rows = tokens.shape[1]
    block = rows // 2
    half_ctx = n_ctx // 2
    capacity = min(rows, 4 * rows * TOP // (3 * n_ctx))
    order_a, order_b = spread_orders()
    reduce_a, reduce_b = order_a[::-1], order_b[::-1]

    tok = tokens[0]
    cot = cotangent[0]
    tok_all = wt_rows(tok)
    cot_all = wt_rows(cot)
    kv_down = wt_gather(w_kv_down, 0)
    kv_up = wt_gather(w_kv_up, 0)
    gains = jnp.stack(
        [gain_attn, gain_mlp, jnp.pad(gain_kv, (0, gain_attn.shape[0] - gain_kv.shape[0]))]
    ).astype(F32)
    gains = wt_gather(gains[None], 0)
    gain_one = gains[:, 0].reshape(1, D).astype(F32)
    gain_two = gains[:, 1].reshape(1, D).astype(F32)
    gain_latent = gains[:, 2, : gain_kv.shape[0]].reshape(1, R).astype(F32)

    place, start = token_places(block_deal, lengths[0], 2 * c, rows, block)
    position = place - start
    frequency = jnp.exp(
        jnp.arange(DR // 2, dtype=F32) * (-2.0 * math.log(10000.0) / DR)
    )
    angles = position.astype(F32)[:, None] * frequency[None, :]
    cos, sin = jnp.cos(angles), jnp.sin(angles)
    lo, hi = start[:, None], place[:, None]
    blocks = jnp.stack(
        [
            jnp.take(block_deal, 2 * (c ^ jnp.array(masks_of(order), jnp.int32)) + side)
            for side, order in ((0, order_a), (1, order_b))
        ]
    )

    inputs_all = tok_all.astype(F32)
    inputs = inputs_all[:rows]
    normed_one = rms_norm(inputs_all, gain_one).astype(BF)
    kv = contract(normed_one[:rows], kv_down, 1, 0)
    latent_raw = kv[:, :R]
    latent = rms_norm(latent_raw, gain_latent).astype(BF)
    first, second = kv[:, R : R + DR // 2], kv[:, R + DR // 2 :]
    own_keys = jnp.concatenate(
        [latent, (first * cos - second * sin).astype(BF), (first * sin + second * cos).astype(BF)],
        axis=1,
    )
    keys_a = ctx_spread(own_keys[:block], order_a)
    keys_b = ctx_spread(own_keys[block:], order_b)
    query = wt_sum_rows(contract(my_part(normed_one, 1), w_query, 1, 0))
    up3 = kv_up.reshape(R, H, DN + DV)
    up_key, up_value = up3[:, :, :DN], up3[:, :, DN:]
    query_nope, query_cat = query_parts(query, cos, sin, up_key)

    partner = functools.partial(ctx_swap, mask=half_ctx)
    route_own = routes[0]
    gate_own = gate_weights[0]
    place_own, high_own, low_own = route_matrices(route_own, gate_own, capacity)
    place_other, high_other, low_other = route_matrices(
        partner(route_own.astype(F32)).astype(jnp.int32), partner(gate_own), capacity
    )
    def swap_blocks(x):
        return jnp.concatenate([x[:1]] + [ctx_swap(x[j : j + 1], j) for j in range(1, half_ctx)], axis=0)

    def to_experts(own, other):
        both = jnp.concatenate(
            [own.reshape(half_ctx, capacity, D), other.reshape(half_ctx, capacity, D)], axis=1
        )
        return swap_blocks(both).reshape(-1, D)

    def from_experts(x):
        x = swap_blocks(x.reshape(half_ctx, 2 * capacity, D))
        return x[:, :capacity].reshape(-1, D), x[:, capacity:].reshape(-1, D)

    cot_other = partner(cot)
    rows_grad = to_experts(
        (contract(high_own, cot, 1, 0) + contract(low_own, cot, 1, 0)).astype(BF),
        (contract(high_other, cot_other, 1, 0) + contract(low_other, cot_other, 1, 0)).astype(BF),
    )

    keys = jnp.concatenate([keys_a, keys_b], axis=0)
    key_place = (blocks[:, :, None] * block + jnp.arange(block, dtype=jnp.int32)).reshape(1, -1)
    seen = (key_place >= lo) & (key_place <= hi)
    out_latent, log_total, heads_out = attend(query_cat, keys, seen, up_value)
    heads_all = wt_rows(heads_out)
    residual = inputs + wt_sum_rows(contract(my_part(heads_all, 1), w_out, 1, 0))
    normed_two = rms_norm(residual, gain_two).astype(BF)

    normed_other = partner(normed_two)
    rows_in = to_experts(
        contract(place_own, normed_two, 1, 0).astype(BF),
        contract(place_other, normed_other, 1, 0).astype(BF),
    )

    two_all = wt_rows(normed_two)
    two_part = my_part(two_all, 1)
    shared_gate = wt_sum_part(contract(two_part, w_shared_gate, 1, 0), 1)
    shared_up = wt_sum_part(contract(two_part, w_shared_up, 1, 0), 1)
    act, slope = silu_parts(shared_gate)
    hidden = (act * shared_up).astype(BF)
    shared_out = wt_sum_rows(contract(hidden, w_shared_down, 1, 0))
    grad_hidden = contract(cot_all, w_shared_down, 1, 1)
    grad_gate = wt_all_columns((grad_hidden * shared_up * slope).astype(BF))
    grad_up = wt_all_columns((grad_hidden * act).astype(BF))
    hidden_all = wt_all_columns(hidden)
    shared_back = wt_own_rows(
        contract(grad_gate, w_shared_gate, 1, 1) + contract(grad_up, w_shared_up, 1, 1)
    )

    def chosen_columns(x):
        wide = x.shape[1] // (n_ctx * n_wt)
        view = x.reshape(x.shape[0], n_ctx, n_wt, wide)
        return my_part(view, 2).reshape(x.shape[0], n_ctx * wide)

    def weight_grad(chunked, other, order):
        grad = contract(chosen_columns(chunked), other, 0, 0).astype(BF)
        return ctx_reduce(grad.reshape(n_ctx, -1, other.shape[1]), order)

    grad_w_shared_gate = weight_grad(two_all, grad_gate, reduce_a)
    grad_w_shared_up = weight_grad(two_all, grad_up, reduce_b)
    grad_w_shared_down = weight_grad(cot_all, hidden_all, reduce_b).T

    gate_matrix = lax.all_gather(w_expert_gate[0], "wt", axis=0, tiled=True)
    up_matrix = lax.all_gather(w_expert_up[0], "wt", axis=0, tiled=True)
    down_matrix = lax.all_gather(w_expert_down[0], "wt", axis=0, tiled=True)
    expert_gate = contract(rows_in, gate_matrix, 1, 0)
    expert_up = contract(rows_in, up_matrix, 1, 0)
    expert_act, expert_slope = silu_parts(expert_gate)
    expert_hidden = (expert_act * expert_up).astype(BF)
    grad_expert_hidden = contract(rows_grad, down_matrix, 1, 1)
    grad_expert_gate = (grad_expert_hidden * expert_up * expert_slope).astype(BF)
    grad_expert_up = (grad_expert_hidden * expert_act).astype(BF)
    grad_rows = (
        contract(grad_expert_gate, gate_matrix, 1, 1) + contract(grad_expert_up, up_matrix, 1, 1)
    ).astype(BF)
    back_own, back_other = from_experts(grad_rows)
    grad_routed = contract(place_own, back_own, 0, 0) + partner(
        contract(place_other, back_other, 0, 0).astype(BF)
    ).astype(F32)
    produced = contract(expert_hidden, down_matrix, 1, 0).astype(BF)
    out_own, out_other = from_experts(produced)
    routed = (
        contract(high_own, out_own, 0, 0)
        + contract(low_own, out_own, 0, 0)
        + partner(
            (contract(high_other, out_other, 0, 0) + contract(low_other, out_other, 0, 0)).astype(BF)
        ).astype(F32)
    )
    mixed_out = (residual + shared_out + routed).astype(BF)

    def expert_sum(grad):
        total = my_part(grad, 0)
        for step in range(1, n_wt):
            w = lax.axis_index("wt")
            total = total + wt_to(part_of(grad, (w + step) % n_wt, 0).astype(BF), step).astype(F32)
        return total[None]

    grad_w_expert_gate = expert_sum(contract(rows_in, grad_expert_gate, 0, 0))
    grad_w_expert_up = expert_sum(contract(rows_in, grad_expert_up, 0, 0))
    grad_w_expert_down = expert_sum(contract(expert_hidden, rows_grad, 0, 0))

    grad_two = shared_back + grad_routed
    grad_part, grad_gain_mlp = rms_back(residual, gain_two, grad_two)
    grad_residual = cot.astype(F32) + grad_part
    grad_attn = wt_rows(grad_residual.astype(BF))
    grad_heads = wt_own_rows(contract(grad_attn, w_out, 1, 1).astype(BF))
    grad_w_out = weight_grad(grad_attn, heads_all, reduce_a).T

    grad_query, grad_query_latent, grad_keys = attend_back(
        query_cat, keys, seen, up_key, up_value, out_latent, log_total, grad_heads, cos, sin
    )
    grad_keys_a, grad_keys_b = jnp.split(grad_keys, 2, axis=0)
    grad_keys = jnp.concatenate(
        [ctx_unspread(grad_keys_a, order_a), ctx_unspread(grad_keys_b, order_b)], axis=0
    )
    grad_up_key = jnp.einsum(
        "thd,htr->hdr", query_nope, grad_query_latent, preferred_element_type=F32
    )
    grad_up_value = jnp.einsum(
        "thv,htr->hvr", grad_heads.reshape(rows, H, DV), out_latent.astype(BF), preferred_element_type=F32
    )
    up_grads = jnp.concatenate([grad_up_key, grad_up_value], axis=1).astype(BF)
    up_grads = up_grads.reshape(n_ctx, n_wt, -1, R)
    own_up = my_part(up_grads, 1).astype(F32)
    for step in range(1, n_wt):
        w = lax.axis_index("wt")
        own_up = own_up + wt_to(part_of(up_grads, (w + step) % n_wt, 1), step).astype(F32)
    grad_w_kv_up = ctx_reduce(own_up.astype(BF).reshape(n_ctx, -1, R), reduce_b).T

    query_all = wt_rows(grad_query)
    query_columns = chosen_columns(query_all)
    grad_w_query = jnp.concatenate(
        [
            ctx_reduce(
                contract(query_columns, normed_one[:, part * (D // 2) : (part + 1) * (D // 2)], 0, 0)
                .astype(BF)
                .reshape(n_ctx, -1, D // 2),
                order,
            ).T
            for part, order in ((0, reduce_a), (1, reduce_b))
        ],
        axis=0,
    )
    one_part = contract(query_all, w_query, 1, 1)

    grad_latent, grad_gain_kv = rms_back(latent_raw, gain_latent, grad_keys[:, :R])
    first, second = grad_keys[:, R : R + DR // 2], grad_keys[:, R + DR // 2 :]
    grad_kv = jnp.concatenate(
        [grad_latent, first * cos + second * sin, second * cos - first * sin], axis=1
    ).astype(BF)
    grad_kv_all = wt_rows(grad_kv)
    grad_w_kv_down = weight_grad(normed_one, grad_kv_all, reduce_a)
    grad_one = wt_own_rows(one_part + contract(grad_kv_all, w_kv_down, 1, 1))
    grad_inputs, grad_gain_attn = rms_back(inputs, gain_one, grad_one)
    grad_tokens = grad_residual + grad_inputs

    gain_grads = jnp.concatenate(
        [
            g.reshape(n_ctx, n_wt, -1)
            for g in (grad_gain_attn, grad_gain_mlp, grad_gain_kv)
        ],
        axis=2,
    )
    own_gain = my_part(gain_grads, 1)
    for step in range(1, n_wt):
        w = lax.axis_index("wt")
        own_gain = own_gain + wt_to(part_of(gain_grads, (w + step) % n_wt, 1), step)
    gain_total = ctx_reduce(own_gain.reshape(n_ctx, 1, -1), reduce_b, F32)[0]
    wide = D // (n_ctx * n_wt)

    return (
        mixed_out[None],
        grad_tokens[None],
        gain_total[:wide],
        grad_w_query,
        grad_w_kv_down,
        gain_total[2 * wide :],
        grad_w_kv_up,
        grad_w_out,
        gain_total[wide : 2 * wide],
        grad_w_shared_gate,
        grad_w_shared_up,
        grad_w_shared_down,
        grad_w_expert_gate,
        grad_w_expert_up,
        grad_w_expert_down,
    )


def solution(mesh):
    placed = (
        P("wt", "ctx", None),
        P("wt"),
        P("wt", None),
        P("wt", None),
        P("wt"),
        P("wt", None),
        P("wt", None),
        P("wt"),
        P("wt", None),
        P("wt", None),
        P("wt", None),
        P("ctx", "wt", None),
        P("ctx", "wt", None),
        P("ctx", "wt", None),
        P(),
        P("wt", None),
        P("wt", "ctx", None),
        P("wt", "ctx", None),
        P("wt", "ctx", None),
    )
    return jax.shard_map(
        per_device,
        mesh=mesh,
        in_specs=placed,
        out_specs=(
            P("wt", "ctx", None),
            P("wt", "ctx", None),
            P(("ctx", "wt")),
            P(None, ("ctx", "wt")),
            P(("ctx", "wt"), None),
            P(("ctx", "wt")),
            P(None, ("ctx", "wt")),
            P(None, ("ctx", "wt")),
            P(("ctx", "wt")),
            P(("ctx", "wt"), None),
            P(("ctx", "wt"), None),
            P(None, ("ctx", "wt")),
            P("ctx", "wt", None),
            P("ctx", "wt", None),
            P("ctx", "wt", None),
        ),
        check_vma=False,
    )
```

```python
import functools
import math

import jax
import jax.numpy as jnp
from jax import lax
from jax.sharding import PartitionSpec as P

D = 2048
H = 16
DN = 128
DR = 64
DV = 128
R = 512
TOP = 6
DQ = DN + DR
KW = R + DR

EPS = 1e-06
SCALE = 1.0 / math.sqrt(DN + DR)
MASKED = -1e30
BF = jnp.bfloat16
F32 = jnp.float32


def contract(former, latter, former_dim, latter_dim):
    return lax.dot_general(
        former,
        latter,
        (((former_dim,), (latter_dim,)), ((), ())),
        preferred_element_type=F32,
    )


def wt_from(x, step):
    count = lax.axis_size("wt")
    return lax.ppermute(x, "wt", [((i + step) % count, i) for i in range(count)])


def wt_to(x, step):
    count = lax.axis_size("wt")
    return lax.ppermute(x, "wt", [(i, (i + step) % count) for i in range(count)])


def wt_rows(x):
    return jnp.concatenate(
        [x] + [wt_from(x, step) for step in range(1, lax.axis_size("wt"))], axis=0
    )


def in_order(parts, axis):
    count = len(parts)
    w = lax.axis_index("wt")
    if count == 2:
        return jnp.where(
            w == 0, jnp.concatenate(parts, axis), jnp.concatenate(parts[::-1], axis)
        )
    size = parts[0].shape[axis]
    return lax.dynamic_slice_in_dim(
        jnp.concatenate(parts + parts, axis), (count - w) % count * size, count * size, axis
    )


def wt_gather(x, axis):
    return in_order([x] + [wt_from(x, step) for step in range(1, lax.axis_size("wt"))], axis)


def part_of(x, index, axis):
    count = lax.axis_size("wt")
    size = x.shape[axis] // count
    if count == 2 and axis > 0:
        return jnp.where(
            index == 0,
            lax.slice_in_dim(x, 0, size, axis=axis),
            lax.slice_in_dim(x, size, 2 * size, axis=axis),
        )
    return lax.dynamic_slice_in_dim(x, index * size, size, axis)


def my_part(x, axis):
    return part_of(x, lax.axis_index("wt"), axis)


def wt_sum_rows(x, sent=F32):
    count = lax.axis_size("wt")
    rows = x.shape[0] // count
    total = x[:rows]
    for step in range(1, count):
        total = total + wt_to(x[step * rows : (step + 1) * rows].astype(sent), step).astype(F32)
    return total


def wt_sum_parts(arrays):
    count = lax.axis_size("wt")
    w = lax.axis_index("wt")
    rows = arrays[0].shape[0] // count
    total = jnp.concatenate([my_part(x, 1) for x in arrays], axis=1)
    for step in range(1, count):
        sent = jnp.concatenate([part_of(x, (w + step) % count, 1) for x in arrays], axis=1)
        other = wt_to(sent.astype(BF), step).astype(F32)
        total = total + jnp.concatenate([other[step * rows :], other[: step * rows]], axis=0)
    return jnp.split(total, len(arrays), axis=1)


def wt_own_rows(x):
    count = lax.axis_size("wt")
    rows = x.shape[0] // count
    parts = [x[:rows]]
    for step in range(1, count):
        back = count - step
        parts.append(
            lax.ppermute(
                x[back * rows : (back + 1) * rows],
                "wt",
                [((i + step) % count, i) for i in range(count)],
            )
        )
    return in_order(parts, 1)


def wt_all_columns(arrays):
    count = lax.axis_size("wt")
    rows = arrays[0].shape[0] // count
    wide = arrays[0].shape[1]
    merged = jnp.concatenate(arrays, axis=1)
    parts = [[x] for x in arrays]
    for step in range(1, count):
        other = wt_from(merged, step)
        other = jnp.concatenate([other[-step * rows :], other[: -step * rows]], axis=0)
        for number, part in enumerate(parts):
            part.append(other[:, number * wide : (number + 1) * wide])
    return [in_order(part, 1) for part in parts]


def ctx_swap(x, mask):
    count = lax.axis_size("ctx")
    return lax.ppermute(x, "ctx", [(i, i ^ mask) for i in range(count)])


def spread_orders():
    bits = []
    bit = lax.axis_size("ctx") // 2
    while bit:
        bits.append(bit)
        bit //= 2
    return bits, bits[:-2] + [bits[-1], bits[-2]]


def masks_of(order):
    masks = [0]
    for bit in order:
        masks = masks + [m ^ bit for m in masks]
    return masks


def ctx_spread(x, order):
    for bit in order:
        x = jnp.concatenate([x, ctx_swap(x, bit)], axis=0)
    return x


def ctx_unspread(x, order):
    for bit in reversed(order):
        half = x.shape[0] // 2
        x = x[:half] + ctx_swap(x[half:].astype(BF), bit).astype(F32)
    return x


class Order:
    def __init__(self):
        self.signs = []

    def __call__(self, x, *others):
        signs = tuple(lax.slice(o, (0,) * o.ndim, (1,) * o.ndim).reshape(()).astype(F32) for o in others)
        held = lax.optimization_barrier((x,) + signs)
        self.signs += held[1:]
        return held[0]

    def seal(self, x):
        return x + 0.0 * sum(self.signs)


class Reduction:
    def __init__(self, x, order, after):
        self.x = x
        self.after = after
        self.tail = x.shape[1:]
        self.order = list(order)
        self.dims = sorted(order, reverse=True)
        self.kept = None
        self.got = None

    def send(self, *others):
        bit = self.order.pop(0)
        place = self.dims.index(bit)
        before, behind = 2**place, 2 ** (len(self.dims) - place - 1)
        self.dims.pop(place)
        view = self.x.reshape((before, 2, behind) + self.tail)
        mine = (lax.axis_index("ctx") // bit) % 2
        self.kept = lax.dynamic_index_in_dim(view, mine, 1, keepdims=False)
        sent = lax.dynamic_index_in_dim(view, 1 - mine, 1, keepdims=False)
        self.got = ctx_swap(self.after(sent, *others) if others else sent, bit)
        return self

    def take(self, *others):
        got = self.after(self.got, *others) if others else self.got
        total = self.kept.astype(F32) + got.astype(F32)
        self.x = total.reshape((-1,) + self.tail)
        if self.order:
            self.x = self.x.astype(BF)
        return self

    def result(self, *others):
        if self.got is not None:
            self.take(*others)
        while self.order:
            self.send().take()
        return self.x.reshape(self.tail)


def ctx_reduce(x, order, sent=BF):
    c = lax.axis_index("ctx")
    count = x.shape[0]
    tail = x.shape[1:]
    dims = []
    bit = count // 2
    while bit:
        dims.append(bit)
        bit //= 2
    for number, bit in enumerate(order):
        place = dims.index(bit)
        before, after = 2**place, 2 ** (len(dims) - place - 1)
        view = x.reshape((before, 2, after) + tail)
        mine = (c // bit) % 2
        keep = lax.dynamic_index_in_dim(view, mine, 1, keepdims=False)
        send = lax.dynamic_index_in_dim(view, 1 - mine, 1, keepdims=False)
        got = ctx_swap(send, bit)
        total = keep.astype(F32) + got.astype(F32)
        dims.pop(place)
        x = total.reshape((before * after,) + tail)
        if number < len(order) - 1:
            x = x.astype(sent)
    return x.reshape(tail)


def query_parts(q, cos, sin, up_key):
    rows = q.shape[0]
    q = q.reshape(rows, H, DQ)
    nope = q[:, :, :DN].astype(BF)
    first, second = q[:, :, DN : DN + DR // 2], q[:, :, DN + DR // 2 :]
    cos, sin = cos[:, None], sin[:, None]
    latent = jnp.einsum("thd,rhd->htr", nope, up_key, preferred_element_type=F32).astype(BF)
    rotary = jnp.concatenate([first * cos - second * sin, first * sin + second * cos], axis=2)
    return nope, jnp.concatenate([latent, rotary.astype(BF).transpose(1, 0, 2)], axis=2)


def attend(query, keys, seen, up_value):
    scores = jnp.einsum("htr,kr->htk", query, keys, preferred_element_type=F32) * SCALE
    scores = jnp.where(seen, scores, MASKED)
    top = jnp.max(scores, axis=2, keepdims=True)
    probs = jnp.exp(scores - top)
    total = jnp.sum(probs, axis=2, keepdims=True)
    out = jnp.einsum("htk,kr->htr", probs.astype(BF), keys[:, :R], preferred_element_type=F32) / total
    heads = jnp.einsum("htr,rhv->thv", out.astype(BF), up_value, preferred_element_type=F32)
    return out, top + jnp.log(total), heads.reshape(heads.shape[0], H * DV).astype(BF)


def attend_back(query, keys, seen, up_key, up_value, out, log_total, grad_heads, cos, sin, beside):
    rows = query.shape[1]
    scores = jnp.einsum("htr,kr->htk", query, keys, preferred_element_type=F32) * SCALE
    probs = jnp.exp(jnp.where(seen, scores, MASKED) - log_total)
    grad_out = jnp.einsum(
        "thv,rhv->htr", grad_heads.reshape(rows, H, DV), up_value, preferred_element_type=F32
    ).astype(BF)
    delta = jnp.sum(grad_out.astype(F32) * out, axis=2, keepdims=True)
    grad_probs = jnp.einsum("htr,kr->htk", grad_out, keys[:, :R], preferred_element_type=F32)
    grad_scores = (probs * (grad_probs - delta) * SCALE).astype(BF)
    grad_query = jnp.einsum("htk,kr->htr", grad_scores, keys, preferred_element_type=F32)
    grad_keys = jnp.einsum("htk,htr->kr", grad_scores, query, preferred_element_type=F32)
    values_part = jnp.einsum("htk,htr->kr", probs.astype(BF), grad_out, preferred_element_type=F32)
    values_part, beside = lax.optimization_barrier((values_part, beside))
    grad_keys = grad_keys + jnp.pad(values_part, ((0, 0), (0, DR)))
    grad_latent = grad_query[:, :, :R].astype(BF)
    nope = jnp.einsum("htr,rhd->thd", grad_latent, up_key, preferred_element_type=F32)
    first, second = grad_query[:, :, R : R + DR // 2], grad_query[:, :, R + DR // 2 :]
    rotary = jnp.concatenate([first * cos + second * sin, second * cos - first * sin], axis=2)
    grad_q = jnp.concatenate([nope, rotary.transpose(1, 0, 2)], axis=2).reshape(rows, H * DQ)
    return grad_q.astype(BF), grad_latent, grad_keys, beside


def rms_norm(values, gain):
    scale = lax.rsqrt(jnp.mean(values * values, axis=1, keepdims=True) + EPS)
    return values * scale * gain


def rms_back(values, gain, grad):
    scale = lax.rsqrt(jnp.mean(values * values, axis=1, keepdims=True) + EPS)
    scaled = grad * gain
    inner = jnp.mean(values * scaled, axis=1, keepdims=True)
    return scale * scaled - values * (scale * scale * scale * inner), jnp.sum(grad * values * scale, axis=0)


def silu_parts(v):
    sig = jax.nn.sigmoid(v)
    return v * sig, sig * (1.0 + v * (1.0 - sig))


def token_places(block_deal, lengths_row, first_block, rows, block):
    blocks = lax.dynamic_slice_in_dim(block_deal, first_block, 2, 0)
    place = (blocks[:, None] * block + jnp.arange(block, dtype=jnp.int32)[None, :]).reshape(rows)
    ends = jnp.cumsum(lengths_row)
    past = place[:, None] >= ends[None, :]
    start = jnp.sum(jnp.where(past, lengths_row[None, :], 0), axis=1)
    return place, start


def route_matrices(routes, gates, capacity):
    count = lax.axis_size("ctx")
    rows = routes.shape[0]
    half = count // 2
    experts = lax.axis_index("ctx") // half * half + jnp.arange(half, dtype=jnp.int32)
    named = routes[:, :, None] == experts[None, None, :]
    chosen = jnp.any(named, axis=1)
    weight = jnp.sum(jnp.where(named, gates[:, :, None], 0.0), axis=1).T
    earlier = (jnp.arange(rows)[:, None] > jnp.arange(rows)[None, :]).astype(BF)
    rank = contract(chosen.astype(BF), earlier, 0, 1).astype(jnp.int32)
    slots = jnp.arange(capacity, dtype=jnp.int32)
    held = (rank[:, None, :] == slots[None, :, None]) & chosen.T[:, None, :]
    place = held.astype(BF).reshape(-1, rows)
    weighted = jnp.where(held, weight[:, None, :], 0.0).reshape(-1, rows)
    high = weighted.astype(BF)
    low = (weighted - high.astype(F32)).astype(BF)
    return place, high, low


def per_device(
    tokens,
    gain_attn,
    w_query,
    w_kv_down,
    gain_kv,
    w_kv_up,
    w_out,
    gain_mlp,
    w_shared_gate,
    w_shared_up,
    w_shared_down,
    w_expert_gate,
    w_expert_up,
    w_expert_down,
    block_deal,
    lengths,
    routes,
    gate_weights,
    cotangent,
):
    n_ctx = lax.axis_size("ctx")
    n_wt = lax.axis_size("wt")
    c = lax.axis_index("ctx")
    rows = tokens.shape[1]
    block = rows // 2
    half_ctx = n_ctx // 2
    capacity = min(rows, 4 * rows * TOP // (3 * n_ctx))
    after = Order()
    order_a, order_b = spread_orders()
    reduce_a, reduce_b = order_a[::-1], order_b[::-1]

    tok = tokens[0]
    cot = cotangent[0]
    kv_down = wt_gather(w_kv_down.T, 1)
    gains = jnp.stack(
        [gain_attn, gain_mlp, jnp.pad(gain_kv, (0, gain_attn.shape[0] - gain_kv.shape[0]))]
    ).astype(F32)
    gains = wt_gather(gains[None], 0)
    gain_one = gains[:, 0].reshape(1, D).astype(F32)
    gain_two = gains[:, 1].reshape(1, D).astype(F32)
    gain_latent = gains[:, 2, : gain_kv.shape[0]].reshape(1, R).astype(F32)

    place, start = token_places(block_deal, lengths[0], 2 * c, rows, block)
    position = place - start
    frequency = jnp.exp(
        jnp.arange(DR // 2, dtype=F32) * (-2.0 * math.log(10000.0) / DR)
    )
    angles = position.astype(F32)[:, None] * frequency[None, :]
    cos, sin = jnp.cos(angles), jnp.sin(angles)
    lo, hi = start[:, None], place[:, None]
    blocks = jnp.stack(
        [
            jnp.take(block_deal, 2 * (c ^ jnp.array(masks_of(order), jnp.int32)) + side)
            for side, order in ((0, order_a), (1, order_b))
        ]
    )

    inputs = tok.astype(F32)
    one_own = rms_norm(inputs, gain_one).astype(BF)
    kv = contract(one_own, kv_down, 1, 1)
    latent_raw = kv[:, :R]
    latent = rms_norm(latent_raw, gain_latent).astype(BF)
    first, second = kv[:, R : R + DR // 2], kv[:, R + DR // 2 :]
    own_keys = jnp.concatenate(
        [latent, (first * cos - second * sin).astype(BF), (first * sin + second * cos).astype(BF)],
        axis=1,
    )
    keys_a = ctx_spread(own_keys[:block], order_a)
    keys_b = ctx_spread(own_keys[block:], order_b)
    tok_all = wt_rows(after(tok, own_keys))
    cot_all = wt_rows(after(cot, own_keys))
    kv_up = wt_gather(after(w_kv_up, own_keys), 0)
    one_part = my_part(rms_norm(tok_all.astype(F32), gain_one).astype(BF), 1)
    query = wt_sum_rows(contract(one_part, w_query, 1, 0), BF)
    up3 = kv_up.reshape(R, H, DN + DV)
    up_key, up_value = up3[:, :, :DN], up3[:, :, DN:]
    query_nope, query_cat = query_parts(query, cos, sin, up_key)

    partner = functools.partial(ctx_swap, mask=half_ctx)
    route_own = routes[0]
    gate_own = gate_weights[0]
    place_own, high_own, low_own = route_matrices(route_own, gate_own, capacity)
    place_other, high_other, low_other = route_matrices(
        partner(route_own.astype(F32)).astype(jnp.int32), partner(gate_own), capacity
    )
    groups = [list(range(half_ctx)), list(range(half_ctx, n_ctx))]

    def swap_blocks(x):
        return lax.all_to_all(x, "ctx", 0, 0, axis_index_groups=groups, tiled=True)

    def slots(x):
        return x.astype(BF).reshape(half_ctx, capacity, D)

    cot_other = partner(cot)
    rows_grad = jnp.concatenate(
        [
            slots(contract(high_own, cot, 1, 0) + contract(low_own, cot, 1, 0)),
            slots(contract(high_other, cot_other, 1, 0) + contract(low_other, cot_other, 1, 0)),
        ],
        axis=1,
    )
    rows_grad = swap_blocks(after(rows_grad, keys_a, keys_b))

    keys = jnp.concatenate([keys_a, keys_b], axis=0)
    key_place = (blocks[:, :, None] * block + jnp.arange(block, dtype=jnp.int32)).reshape(1, -1)
    seen = (key_place >= lo) & (key_place <= hi)
    out_latent, log_total, heads_out = attend(query_cat, keys, seen, up_value)
    heads_all = wt_rows(heads_out)
    residual = inputs + wt_sum_rows(contract(my_part(heads_all, 1), w_out, 1, 0))
    normed_two = rms_norm(residual, gain_two).astype(BF)
    normed_two, rows_grad = lax.optimization_barrier((normed_two, rows_grad))
    grad_own, grad_other = rows_grad[:, :capacity].reshape(-1, D), rows_grad[:, capacity:].reshape(-1, D)

    rows_own = swap_blocks(slots(contract(place_own, normed_two, 1, 0))).reshape(-1, D)
    normed_other = partner(normed_two)
    rows_other = swap_blocks(slots(contract(place_other, normed_other, 1, 0))).reshape(-1, D)

    two_all = wt_rows(normed_two)
    two_part = my_part(two_all, 1)
    shared_gate, shared_up = wt_sum_parts(
        [contract(two_part, w_shared_gate, 1, 0), contract(two_part, w_shared_up, 1, 0)]
    )
    act, slope = silu_parts(shared_gate)
    hidden = (act * shared_up).astype(BF)
    shared_out = wt_sum_rows(contract(hidden, w_shared_down, 1, 0))
    grad_hidden = contract(cot_all, w_shared_down, 1, 1)
    grad_gate, grad_up, hidden_all = wt_all_columns(
        [(grad_hidden * shared_up * slope).astype(BF), (grad_hidden * act).astype(BF), hidden]
    )
    shared_back = wt_own_rows(
        contract(grad_gate, w_shared_gate, 1, 1) + contract(grad_up, w_shared_up, 1, 1)
    )

    def pair_send(chunked, other, bit, *others):
        mine = (c // bit) % 2
        view = chunked.reshape(rows, half_ctx // bit, 2, -1)
        keep = jnp.where(mine == 0, view[:, :, 0], view[:, :, 1]).reshape(rows, -1)
        sent = jnp.where(mine == 0, view[:, :, 1], view[:, :, 0]).reshape(rows, -1)
        got = ctx_swap(after(jnp.concatenate([sent, other], axis=1), *others), bit)
        return jnp.concatenate([jnp.concatenate([keep, other], axis=1), got], axis=0), keep.shape[1]

    def pair_grad(sent, *others):
        both, wide = sent
        both = wt_rows(after(both, *others))
        columns, partners = both[:, :wide], both[:, wide:]
        columns = my_part(columns.reshape(-1, half_ctx, n_wt, wide // (half_ctx * n_wt)), 2).reshape(-1, wide // n_wt)
        grad = contract(columns, partners, 0, 0).astype(BF)
        return grad.reshape(half_ctx, -1, partners.shape[1])

    def scatter_sum(x, bit):
        sides = [[i for i in range(n_ctx) if i // bit % 2 == side] for side in range(2)]
        return lax.psum_scatter(x, "ctx", scatter_dimension=0, axis_index_groups=sides, tiled=True)[0].astype(F32)

    gate_matrix = lax.all_gather(w_expert_gate[0], "wt", axis=0, tiled=True)
    up_matrix = lax.all_gather(w_expert_up[0], "wt", axis=0, tiled=True)
    down_matrix = lax.all_gather(w_expert_down[0], "wt", axis=0, tiled=True)

    def expert(rows_in, rows_grad):
        gate = contract(rows_in, gate_matrix, 1, 0)
        up = contract(rows_in, up_matrix, 1, 0)
        gate_act, gate_slope = silu_parts(gate)
        grad_inner = contract(rows_grad, down_matrix, 1, 1)
        grad_gate_pre = (grad_inner * up * gate_slope).astype(BF)
        grad_up_pre = (grad_inner * gate_act).astype(BF)
        grad_in = contract(grad_gate_pre, gate_matrix, 1, 1) + contract(grad_up_pre, up_matrix, 1, 1)
        return (gate_act * up).astype(BF), grad_gate_pre, grad_up_pre, slots(grad_in)

    hidden_1, grad_gate_1, grad_up_1, grad_in_1 = expert(rows_own, grad_own)
    back_own = swap_blocks(grad_in_1).reshape(-1, D)
    hidden_2, grad_gate_2, grad_up_2, grad_in_2 = expert(after(rows_other, grad_in_1), grad_other)
    sent_gate_up = pair_send(
        normed_two, jnp.concatenate([grad_gate[:rows], grad_up[:rows]], axis=1), reduce_a[0], grad_in_1
    )
    sent_down = pair_send(cot, hidden_all[:rows], reduce_b[0], grad_in_1)
    grad_in_2, back_own = lax.optimization_barrier((grad_in_2, back_own))
    back_other = swap_blocks(grad_in_2).reshape(-1, D)
    grads_gate_up = pair_grad(sent_gate_up, grad_in_2)
    grads_down = pair_grad(sent_down, grad_in_2)
    sums_gate_up = scatter_sum(grads_gate_up, reduce_a[0])
    sums_down = scatter_sum(grads_down, reduce_b[0])
    produced = jnp.concatenate(
        [slots(contract(after(x, grad_in_2), down_matrix, 1, 0)) for x in (hidden_1, hidden_2)], axis=1
    )
    grad_routed = contract(place_own, back_own, 0, 0) + partner(
        contract(place_other, back_other, 0, 0).astype(BF)
    ).astype(F32)

    def expert_sum(grad):
        total = my_part(grad, 0)
        for step in range(1, n_wt):
            w = lax.axis_index("wt")
            total = total + wt_to(part_of(grad, (w + step) % n_wt, 0).astype(BF), step).astype(F32)
        return total[None]

    grad_two = shared_back + grad_routed
    grad_part, grad_gain_mlp = rms_back(residual, gain_two, grad_two)
    grad_residual = cot.astype(F32) + grad_part
    grad_attn_own = grad_residual.astype(BF)
    grad_attn = wt_rows(grad_attn_own)
    grad_heads = wt_own_rows(contract(grad_attn, w_out, 1, 1).astype(BF))
    sent_out = pair_send(grad_attn_own, heads_out, reduce_b[0], grad_heads)

    out_rows = swap_blocks(after(produced, grad_routed))

    grad_query, grad_query_latent, grad_keys, out_rows = attend_back(
        query_cat, keys, seen, up_key, up_value, out_latent, log_total, grad_heads, cos, sin, out_rows
    )
    out_own, out_other = out_rows[:, :capacity].reshape(-1, D), out_rows[:, capacity:].reshape(-1, D)
    grad_keys_a, grad_keys_b = jnp.split(grad_keys, 2, axis=0)
    sent_query = [
        pair_send(grad_query, one_own[:, part * (D // 2) : (part + 1) * (D // 2)], order[0], grad_keys_a)
        for part, order in ((0, reduce_a), (1, reduce_b))
    ]
    grad_keys = jnp.concatenate(
        [ctx_unspread(grad_keys_a, order_a), ctx_unspread(grad_keys_b, order_b)], axis=0
    )
    routed = (
        contract(high_own, out_own, 0, 0)
        + contract(low_own, out_own, 0, 0)
        + partner(
            (contract(high_other, out_other, 0, 0) + contract(low_other, out_other, 0, 0)).astype(BF)
        ).astype(F32)
    )
    mixed_out = (residual + shared_out + routed).astype(BF)
    rows_own, rows_other, grad_own, grad_other = (
        after(x, grad_keys_a) for x in (rows_own, rows_other, grad_own, grad_other)
    )
    rows_in = jnp.concatenate([rows_own, rows_other], axis=0)
    expert_hidden = jnp.concatenate([hidden_1, hidden_2], axis=0)
    rows_grad = jnp.concatenate([grad_own, grad_other], axis=0)
    grad_w_expert_gate = expert_sum(contract(rows_in, jnp.concatenate([grad_gate_1, grad_gate_2], axis=0), 0, 0))
    grad_w_expert_up = expert_sum(contract(rows_in, jnp.concatenate([grad_up_1, grad_up_2], axis=0), 0, 0))
    grad_w_expert_down = expert_sum(contract(expert_hidden, rows_grad, 0, 0))

    grad_up_key = jnp.einsum(
        "thd,htr->hdr", query_nope, grad_query_latent, preferred_element_type=F32
    )
    grad_up_value = jnp.einsum(
        "thv,htr->hvr", grad_heads.reshape(rows, H, DV), out_latent.astype(BF), preferred_element_type=F32
    )
    up_grads = jnp.concatenate([grad_up_key, grad_up_value], axis=1).astype(BF)
    up_grads = up_grads.reshape(n_ctx, n_wt, -1, R)
    own_up = my_part(up_grads, 1).astype(F32)
    for step in range(1, n_wt):
        w = lax.axis_index("wt")
        own_up = own_up + wt_to(part_of(up_grads, (w + step) % n_wt, 1), step).astype(F32)
    sum_kv_up = Reduction(own_up.astype(BF).reshape(n_ctx, -1, R), reduce_a, after)

    query_all = wt_rows(grad_query)
    sum_out = Reduction(pair_grad(sent_out, grad_keys_a), reduce_b[1:], after).send()
    sums_query = [
        Reduction(pair_grad(sent, grad_keys), order[1:], after).send()
        for sent, order in zip(sent_query, (reduce_a, reduce_b))
    ]
    sum_kv_up.send(grad_keys)
    one_back = contract(query_all, w_query, 1, 1)

    grad_latent, grad_gain_kv = rms_back(latent_raw, gain_latent, grad_keys[:, :R])
    first, second = grad_keys[:, R : R + DR // 2], grad_keys[:, R + DR // 2 :]
    grad_kv = jnp.concatenate(
        [grad_latent, first * cos + second * sin, second * cos - first * sin], axis=1
    ).astype(BF)
    grad_kv_all = wt_rows(grad_kv)
    sum_kv_down = Reduction(pair_grad(pair_send(one_own, grad_kv, reduce_b[0], grad_kv)), reduce_b[1:], after)
    grad_one = wt_own_rows(one_back + contract(grad_kv_all, w_kv_down, 1, 1))
    grad_inputs, grad_gain_attn = rms_back(inputs, gain_one, grad_one)
    grad_tokens = grad_residual + grad_inputs

    gain_grads = jnp.concatenate(
        [
            g.reshape(n_ctx, n_wt, -1)
            for g in (grad_gain_attn, grad_gain_mlp, grad_gain_kv)
        ],
        axis=2,
    )
    own_gain = my_part(gain_grads, 1)
    for step in range(1, n_wt):
        w = lax.axis_index("wt")
        own_gain = own_gain + wt_to(part_of(gain_grads, (w + step) % n_wt, 1), step)
    gain_total = after.seal(ctx_reduce(own_gain.reshape(n_ctx, 1, -1), reduce_b, F32)[0])
    wide = D // (n_ctx * n_wt)
    grad_w_kv_down = sum_kv_down.result()
    grad_w_query = jnp.concatenate([part.result().T for part in sums_query], axis=0)
    grad_w_kv_up = sum_kv_up.result().T
    grad_w_shared_gate, grad_w_shared_up = jnp.split(sums_gate_up, 2, axis=1)
    grad_w_shared_down = sums_down.T
    grad_w_out = sum_out.result().T

    return (
        mixed_out[None],
        grad_tokens[None],
        gain_total[:wide],
        grad_w_query,
        grad_w_kv_down,
        gain_total[2 * wide :],
        grad_w_kv_up,
        grad_w_out,
        gain_total[wide : 2 * wide],
        grad_w_shared_gate,
        grad_w_shared_up,
        grad_w_shared_down,
        grad_w_expert_gate,
        grad_w_expert_up,
        grad_w_expert_down,
    )


def solution(mesh):
    placed = (
        P("wt", "ctx", None),
        P("wt"),
        P("wt", None),
        P("wt", None),
        P("wt"),
        P("wt", None),
        P("wt", None),
        P("wt"),
        P("wt", None),
        P("wt", None),
        P("wt", None),
        P("ctx", "wt", None),
        P("ctx", "wt", None),
        P("ctx", "wt", None),
        P(),
        P("wt", None),
        P("wt", "ctx", None),
        P("wt", "ctx", None),
        P("wt", "ctx", None),
    )
    return jax.shard_map(
        per_device,
        mesh=mesh,
        in_specs=placed,
        out_specs=(
            P("wt", "ctx", None),
            P("wt", "ctx", None),
            P(("ctx", "wt")),
            P(None, ("ctx", "wt")),
            P(("ctx", "wt"), None),
            P(("ctx", "wt")),
            P(None, ("ctx", "wt")),
            P(None, ("ctx", "wt")),
            P(("ctx", "wt")),
            P(("ctx", "wt"), None),
            P(("ctx", "wt"), None),
            P(None, ("ctx", "wt")),
            P("ctx", "wt", None),
            P("ctx", "wt", None),
            P("ctx", "wt", None),
        ),
        check_vma=False,
    )
```

```python
import functools
import math

import jax
import jax.numpy as jnp
from jax import lax
from jax.experimental.layout import Layout, with_layout_constraint
from jax.sharding import PartitionSpec as P

D = 2048
H = 16
DN = 128
DR = 64
DV = 128
R = 512
TOP = 6
DQ = DN + DR
KW = R + DR

EPS = 1e-06
SCALE = 1.0 / math.sqrt(DN + DR)
MASKED = -1e30
BF = jnp.bfloat16
F32 = jnp.float32


def contract(former, latter, former_dim, latter_dim):
    return lax.dot_general(
        former,
        latter,
        (((former_dim,), (latter_dim,)), ((), ())),
        preferred_element_type=F32,
    )


def wt_from(x, step):
    count = lax.axis_size("wt")
    return lax.ppermute(x, "wt", [((i + step) % count, i) for i in range(count)])


def wt_to(x, step):
    count = lax.axis_size("wt")
    return lax.ppermute(x, "wt", [(i, (i + step) % count) for i in range(count)])


def wt_rows(x):
    return jnp.concatenate(
        [x] + [wt_from(x, step) for step in range(1, lax.axis_size("wt"))], axis=0
    )


def in_order(parts, axis):
    count = len(parts)
    w = lax.axis_index("wt")
    if count == 2:
        return jnp.where(
            w == 0, jnp.concatenate(parts, axis), jnp.concatenate(parts[::-1], axis)
        )
    size = parts[0].shape[axis]
    return lax.dynamic_slice_in_dim(
        jnp.concatenate(parts + parts, axis), (count - w) % count * size, count * size, axis
    )


def wt_gather(x, axis):
    return in_order([x] + [wt_from(x, step) for step in range(1, lax.axis_size("wt"))], axis)


def part_of(x, index, axis):
    count = lax.axis_size("wt")
    size = x.shape[axis] // count
    if count == 2 and axis > 0:
        return jnp.where(
            index == 0,
            lax.slice_in_dim(x, 0, size, axis=axis),
            lax.slice_in_dim(x, size, 2 * size, axis=axis),
        )
    return lax.dynamic_slice_in_dim(x, index * size, size, axis)


def my_part(x, axis):
    return part_of(x, lax.axis_index("wt"), axis)


def wt_sum_rows(x, sent=F32):
    count = lax.axis_size("wt")
    rows = x.shape[0] // count
    total = x[:rows]
    for step in range(1, count):
        total = total + wt_to(x[step * rows : (step + 1) * rows].astype(sent), step).astype(F32)
    return total


def wt_sum_parts(arrays):
    count = lax.axis_size("wt")
    w = lax.axis_index("wt")
    rows = arrays[0].shape[0] // count
    total = jnp.concatenate([my_part(x, 1) for x in arrays], axis=1)
    for step in range(1, count):
        sent = jnp.concatenate([part_of(x, (w + step) % count, 1) for x in arrays], axis=1)
        other = wt_to(sent.astype(BF), step).astype(F32)
        total = total + jnp.concatenate([other[step * rows :], other[: step * rows]], axis=0)
    return jnp.split(total, len(arrays), axis=1)


def wt_own_rows(x):
    count = lax.axis_size("wt")
    rows = x.shape[0] // count
    parts = [x[:rows]]
    for step in range(1, count):
        back = count - step
        parts.append(
            lax.ppermute(
                x[back * rows : (back + 1) * rows],
                "wt",
                [((i + step) % count, i) for i in range(count)],
            )
        )
    return in_order(parts, 1)


def wt_all_columns(arrays):
    count = lax.axis_size("wt")
    rows = arrays[0].shape[0] // count
    wide = arrays[0].shape[1]
    merged = jnp.concatenate(arrays, axis=1)
    parts = [[x] for x in arrays]
    for step in range(1, count):
        other = wt_from(merged, step)
        other = jnp.concatenate([other[-step * rows :], other[: -step * rows]], axis=0)
        for number, part in enumerate(parts):
            part.append(other[:, number * wide : (number + 1) * wide])
    return [in_order(part, 1) for part in parts]


def ctx_swap(x, mask):
    count = lax.axis_size("ctx")
    return lax.ppermute(x, "ctx", [(i, i ^ mask) for i in range(count)])


def spread_orders():
    bits = []
    bit = lax.axis_size("ctx") // 2
    while bit:
        bits.append(bit)
        bit //= 2
    return bits, bits[:-2] + [bits[-1], bits[-2]]


def masks_of(order):
    masks = [0]
    for bit in order:
        masks = masks + [m ^ bit for m in masks]
    return masks


def ctx_spread(x, order):
    for bit in order:
        x = jnp.concatenate([x, ctx_swap(x, bit)], axis=0)
    return x


def ctx_unspread(x, order):
    for bit in reversed(order):
        half = x.shape[0] // 2
        x = x[:half] + ctx_swap(x[half:].astype(BF), bit).astype(F32)
    return x


class Order:
    def __init__(self):
        self.signs = []

    def __call__(self, x, *others):
        signs = tuple(lax.slice(o, (0,) * o.ndim, (1,) * o.ndim).reshape(()).astype(F32) for o in others)
        held = lax.optimization_barrier((x,) + signs)
        self.signs += held[1:]
        return held[0]

    def seal(self, x):
        return x + 0.0 * sum(self.signs)


class Reduction:
    def __init__(self, x, order, after):
        self.x = x
        self.after = after
        self.tail = x.shape[1:]
        self.order = list(order)
        self.dims = sorted(order, reverse=True)
        self.kept = None
        self.got = None

    def send(self, *others):
        bit = self.order.pop(0)
        place = self.dims.index(bit)
        before, behind = 2**place, 2 ** (len(self.dims) - place - 1)
        self.dims.pop(place)
        view = self.x.reshape((before, 2, behind) + self.tail)
        mine = (lax.axis_index("ctx") // bit) % 2
        self.kept = lax.dynamic_index_in_dim(view, mine, 1, keepdims=False)
        sent = lax.dynamic_index_in_dim(view, 1 - mine, 1, keepdims=False)
        self.got = ctx_swap(self.after(sent, *others) if others else sent, bit)
        return self

    def take(self, *others):
        got = self.after(self.got, *others) if others else self.got
        total = self.kept.astype(F32) + got.astype(F32)
        self.x = total.reshape((-1,) + self.tail)
        if self.order:
            self.x = self.x.astype(BF)
        return self

    def result(self, *others):
        if self.got is not None:
            self.take(*others)
        while self.order:
            self.send().take()
        return self.x.reshape(self.tail)


def ctx_reduce(x, order, sent=BF):
    c = lax.axis_index("ctx")
    count = x.shape[0]
    tail = x.shape[1:]
    dims = []
    bit = count // 2
    while bit:
        dims.append(bit)
        bit //= 2
    for number, bit in enumerate(order):
        place = dims.index(bit)
        before, after = 2**place, 2 ** (len(dims) - place - 1)
        view = x.reshape((before, 2, after) + tail)
        mine = (c // bit) % 2
        keep = lax.dynamic_index_in_dim(view, mine, 1, keepdims=False)
        send = lax.dynamic_index_in_dim(view, 1 - mine, 1, keepdims=False)
        got = ctx_swap(send, bit)
        total = keep.astype(F32) + got.astype(F32)
        dims.pop(place)
        x = total.reshape((before * after,) + tail)
        if number < len(order) - 1:
            x = x.astype(sent)
    return x.reshape(tail)


def query_parts(q, cos, sin, up_key):
    rows = q.shape[0]
    q = q.reshape(rows, H, DQ)
    nope = q[:, :, :DN].astype(BF)
    first, second = q[:, :, DN : DN + DR // 2], q[:, :, DN + DR // 2 :]
    cos, sin = cos[:, None], sin[:, None]
    latent = jnp.einsum("thd,rhd->htr", nope, up_key, preferred_element_type=F32).astype(BF)
    rotary = jnp.concatenate([first * cos - second * sin, first * sin + second * cos], axis=2)
    return nope, jnp.concatenate([latent, rotary.astype(BF).transpose(1, 0, 2)], axis=2)


def attend(query, keys, seen, up_value):
    scores = jnp.einsum("htr,kr->htk", query, keys, preferred_element_type=F32) * SCALE
    scores = jnp.where(seen, scores, MASKED)
    top = jnp.max(scores, axis=2, keepdims=True)
    probs = jnp.exp(scores - top)
    total = jnp.sum(probs, axis=2, keepdims=True)
    out = jnp.einsum("htk,kr->htr", probs.astype(BF), keys[:, :R], preferred_element_type=F32) / total
    heads = jnp.einsum("htr,rhv->thv", out.astype(BF), up_value, preferred_element_type=F32)
    return out, top + jnp.log(total), heads.reshape(heads.shape[0], H * DV).astype(BF)


def attend_back(query, keys, seen, up_key, up_value, out, log_total, grad_heads, cos, sin):
    rows = query.shape[1]
    scores = jnp.einsum("htr,kr->htk", query, keys, preferred_element_type=F32) * SCALE
    probs = jnp.exp(jnp.where(seen, scores, MASKED) - log_total)
    grad_out = jnp.einsum(
        "thv,rhv->htr", grad_heads.reshape(rows, H, DV), up_value, preferred_element_type=F32
    ).astype(BF)
    delta = jnp.sum(grad_out.astype(F32) * out, axis=2, keepdims=True)
    grad_probs = jnp.einsum("htr,kr->htk", grad_out, keys[:, :R], preferred_element_type=F32)
    grad_scores = (probs * (grad_probs - delta) * SCALE).astype(BF)
    grad_query = jnp.einsum("htk,kr->htr", grad_scores, keys, preferred_element_type=F32)
    grad_keys = jnp.einsum("htk,htr->kr", grad_scores, query, preferred_element_type=F32)
    values_part = jnp.einsum("htk,htr->kr", probs.astype(BF), grad_out, preferred_element_type=F32)
    grad_keys = grad_keys + jnp.pad(values_part, ((0, 0), (0, DR)))
    grad_latent = grad_query[:, :, :R].astype(BF)
    nope = jnp.einsum("htr,rhd->thd", grad_latent, up_key, preferred_element_type=F32)
    first, second = grad_query[:, :, R : R + DR // 2], grad_query[:, :, R + DR // 2 :]
    rotary = jnp.concatenate([first * cos + second * sin, second * cos - first * sin], axis=2)
    grad_q = jnp.concatenate([nope, rotary.transpose(1, 0, 2)], axis=2).reshape(rows, H * DQ)
    return grad_q.astype(BF), grad_latent, grad_keys


def rms_norm(values, gain):
    scale = lax.rsqrt(jnp.mean(values * values, axis=1, keepdims=True) + EPS)
    return values * scale * gain


def rms_back(values, gain, grad):
    scale = lax.rsqrt(jnp.mean(values * values, axis=1, keepdims=True) + EPS)
    scaled = grad * gain
    inner = jnp.mean(values * scaled, axis=1, keepdims=True)
    return scale * scaled - values * (scale * scale * scale * inner), jnp.sum(grad * values * scale, axis=0)


def silu_parts(v):
    sig = jax.nn.sigmoid(v)
    return v * sig, sig * (1.0 + v * (1.0 - sig))


def token_places(block_deal, lengths_row, first_block, rows, block):
    blocks = lax.dynamic_slice_in_dim(block_deal, first_block, 2, 0)
    place = (blocks[:, None] * block + jnp.arange(block, dtype=jnp.int32)[None, :]).reshape(rows)
    ends = jnp.cumsum(lengths_row)
    past = place[:, None] >= ends[None, :]
    start = jnp.sum(jnp.where(past, lengths_row[None, :], 0), axis=1)
    return place, start


def route_matrices(routes, gates, capacity):
    count = lax.axis_size("ctx")
    rows = routes.shape[0]
    half = count // 2
    experts = lax.axis_index("ctx") // half * half + jnp.arange(half, dtype=jnp.int32)
    named = routes[:, :, None] == experts[None, None, :]
    chosen = jnp.any(named, axis=1)
    weight = jnp.sum(jnp.where(named, gates[:, :, None], 0.0), axis=1).T
    earlier = (jnp.arange(rows)[:, None] > jnp.arange(rows)[None, :]).astype(BF)
    rank = contract(chosen.astype(BF), earlier, 0, 1).astype(jnp.int32)
    slots = jnp.arange(capacity, dtype=jnp.int32)
    held = (rank[:, None, :] == slots[None, :, None]) & chosen.T[:, None, :]
    place = held.astype(BF).reshape(-1, rows)
    weighted = jnp.where(held, weight[:, None, :], 0.0).reshape(-1, rows)
    high = weighted.astype(BF)
    low = (weighted - high.astype(F32)).astype(BF)
    return place, high, low


def per_device(
    tokens,
    gain_attn,
    w_query,
    w_kv_down,
    gain_kv,
    w_kv_up,
    w_out,
    gain_mlp,
    w_shared_gate,
    w_shared_up,
    w_shared_down,
    w_expert_gate,
    w_expert_up,
    w_expert_down,
    block_deal,
    lengths,
    routes,
    gate_weights,
    cotangent,
):
    n_ctx = lax.axis_size("ctx")
    n_wt = lax.axis_size("wt")
    c = lax.axis_index("ctx")
    rows = tokens.shape[1]
    block = rows // 2
    half_ctx = n_ctx // 2
    capacity = min(rows, 4 * rows * TOP // (3 * n_ctx))
    after = Order()
    partner = functools.partial(ctx_swap, mask=half_ctx)
    order_a, order_b = spread_orders()
    reduce_a, reduce_b = order_a[::-1], order_b[::-1]

    tok = tokens[0]
    cot = cotangent[0]
    kv_down = wt_gather(w_kv_down.T, 1)
    gains = jnp.stack(
        [gain_attn, gain_mlp, jnp.pad(gain_kv, (0, gain_attn.shape[0] - gain_kv.shape[0]))]
    ).astype(F32)
    gains = wt_gather(gains[None], 0)
    gain_one = gains[:, 0].reshape(1, D).astype(F32)
    gain_two = gains[:, 1].reshape(1, D).astype(F32)
    gain_latent = gains[:, 2, : gain_kv.shape[0]].reshape(1, R).astype(F32)

    place, start = token_places(block_deal, lengths[0], 2 * c, rows, block)
    position = place - start
    frequency = jnp.exp(
        jnp.arange(DR // 2, dtype=F32) * (-2.0 * math.log(10000.0) / DR)
    )
    angles = position.astype(F32)[:, None] * frequency[None, :]
    cos, sin = jnp.cos(angles), jnp.sin(angles)
    lo, hi = start[:, None], place[:, None]
    blocks = jnp.stack(
        [
            jnp.take(block_deal, 2 * (c ^ jnp.array(masks_of(order), jnp.int32)) + side)
            for side, order in ((0, order_a), (1, order_b))
        ]
    )

    inputs = tok.astype(F32)
    one_own = rms_norm(inputs, gain_one).astype(BF)
    kv = contract(one_own, kv_down, 1, 1)
    latent_raw = kv[:, :R]
    latent = rms_norm(latent_raw, gain_latent).astype(BF)
    first, second = kv[:, R : R + DR // 2], kv[:, R + DR // 2 :]
    own_keys = jnp.concatenate(
        [latent, (first * cos - second * sin).astype(BF), (first * sin + second * cos).astype(BF)],
        axis=1,
    )
    keys_a = ctx_spread(own_keys[:block], order_a[:1])
    keys_b = ctx_spread(own_keys[block:], order_b[:1])
    cot_other = partner(after(cot, keys_a, keys_b))
    tables = partner(after(jnp.concatenate([routes[0].astype(F32), gate_weights[0]], axis=1), own_keys))
    keys_a = ctx_spread(keys_a, order_a[1:])
    keys_b = ctx_spread(keys_b, order_b[1:])
    tok_all = wt_rows(after(tok, own_keys))
    cot_all = wt_rows(after(cot, own_keys))
    kv_up = with_layout_constraint(wt_gather(after(w_kv_up, own_keys), 0), Layout((0, 1)))
    one_all = rms_norm(tok_all.astype(F32), gain_one).astype(BF)
    one_part = my_part(one_all, 1)
    query = wt_sum_rows(contract(one_part, w_query, 1, 0), BF)
    up3 = kv_up.reshape(R, H, DN + DV)
    up_key, up_value = up3[:, :, :DN], up3[:, :, DN:]
    query_nope, query_cat = query_parts(query, cos, sin, up_key)

    route_own = routes[0]
    gate_own = gate_weights[0]
    place_own, high_own, low_own = route_matrices(route_own, gate_own, capacity)
    place_other, high_other, low_other = route_matrices(
        tables[:, :TOP].astype(jnp.int32), tables[:, TOP:], capacity
    )
    groups = [list(range(half_ctx)), list(range(half_ctx, n_ctx))]

    def swap_blocks(x):
        return lax.all_to_all(x, "ctx", 0, 0, axis_index_groups=groups, tiled=True)

    def slots(x):
        return x.astype(BF).reshape(half_ctx, capacity, D)

    rows_grad = jnp.concatenate(
        [
            slots(contract(high_own, cot, 1, 0) + contract(low_own, cot, 1, 0)),
            slots(contract(high_other, cot_other, 1, 0) + contract(low_other, cot_other, 1, 0)),
        ],
        axis=1,
    )
    rows_grad = swap_blocks(after(rows_grad, keys_a, keys_b))

    keys = jnp.concatenate([keys_a, keys_b], axis=0)
    key_place = (blocks[:, :, None] * block + jnp.arange(block, dtype=jnp.int32)).reshape(1, -1)
    seen = (key_place >= lo) & (key_place <= hi)
    out_latent, log_total, heads_out = attend(query_cat, keys, seen, up_value)
    heads_all = wt_rows(heads_out)
    residual = inputs + wt_sum_rows(contract(my_part(heads_all, 1), w_out, 1, 0))
    normed_two = rms_norm(residual, gain_two).astype(BF)
    normed_two, rows_grad = lax.optimization_barrier((normed_two, rows_grad))
    grad_own, grad_other = rows_grad[:, :capacity].reshape(-1, D), rows_grad[:, capacity:].reshape(-1, D)

    rows_own = swap_blocks(slots(contract(place_own, normed_two, 1, 0))).reshape(-1, D)
    normed_other = partner(normed_two)
    rows_other = swap_blocks(slots(contract(place_other, normed_other, 1, 0))).reshape(-1, D)

    two_all = wt_rows(normed_two)
    two_part = my_part(two_all, 1)
    shared_terms = [contract(two_part, w, 1, 0) for w in (w_shared_gate, w_shared_up)]

    gate_matrix = lax.all_gather(w_expert_gate[0], "wt", axis=0, tiled=True)
    up_matrix = lax.all_gather(w_expert_up[0], "wt", axis=0, tiled=True)
    down_matrix = lax.all_gather(w_expert_down[0], "wt", axis=0, tiled=True)

    def expert(rows_in, rows_grad):
        gate = contract(rows_in, gate_matrix, 1, 0)
        up = contract(rows_in, up_matrix, 1, 0)
        gate_act, gate_slope = silu_parts(gate)
        grad_inner = contract(rows_grad, down_matrix, 1, 1)
        grad_gate_pre = (grad_inner * up * gate_slope).astype(BF)
        grad_up_pre = (grad_inner * gate_act).astype(BF)
        grad_in = contract(grad_gate_pre, gate_matrix, 1, 1) + contract(grad_up_pre, up_matrix, 1, 1)
        return (gate_act * up).astype(BF), grad_gate_pre, grad_up_pre, slots(grad_in)

    hidden_1, grad_gate_1, grad_up_1, grad_in_1 = expert(rows_own, grad_own)
    hidden_2, grad_gate_2, grad_up_2, grad_in_2 = expert(after(rows_other, grad_in_1), grad_other)
    back_own = swap_blocks(grad_in_1).reshape(-1, D)
    grad_in_2, back_own = lax.optimization_barrier((grad_in_2, back_own))
    back_other = swap_blocks(grad_in_2).reshape(-1, D)

    shared_gate, shared_up = wt_sum_parts([after(x, grad_in_2) for x in shared_terms])
    act, slope = silu_parts(shared_gate)
    hidden = (act * shared_up).astype(BF)
    shared_out = wt_sum_rows(contract(hidden, w_shared_down, 1, 0))
    grad_hidden = contract(cot_all, w_shared_down, 1, 1)
    grad_gate, grad_up, hidden_all = wt_all_columns(
        [(grad_hidden * shared_up * slope).astype(BF), (grad_hidden * act).astype(BF), hidden]
    )
    shared_back = wt_own_rows(
        contract(grad_gate, w_shared_gate, 1, 1) + contract(grad_up, w_shared_up, 1, 1)
    )

    def pair_send(chunked, other, bit, *others):
        mine = (c // bit) % 2
        view = chunked.reshape(rows, half_ctx // bit, 2, -1)
        low, high = view[:, :, 0].reshape(rows, -1), view[:, :, 1].reshape(rows, -1)
        keep = jnp.where(mine == 0, low, high)
        sent = jnp.where(mine == 0, high, low)
        got = ctx_swap(after(jnp.concatenate([sent] + other, axis=1), *others), bit)
        return jnp.concatenate([jnp.concatenate([keep] + other, axis=1), got], axis=0)

    def pair_grad(both, deep, *others):
        both = wt_rows(after(both, *others))
        wide = both.shape[1] - deep
        columns, partners = both[:, :wide], both[:, wide:]
        columns = my_part(columns.reshape(-1, half_ctx, n_wt, wide // (half_ctx * n_wt)), 2).reshape(-1, wide // n_wt)
        grad = contract(columns, partners, 0, 0).astype(BF)
        return grad.reshape(half_ctx, -1, deep)

    def scatter_sum(x, bit):
        sides = [[i for i in range(n_ctx) if i // bit % 2 == side] for side in range(2)]
        return lax.psum_scatter(x, "ctx", scatter_dimension=0, axis_index_groups=sides, tiled=True)[0].astype(F32)

    hidden_wide = grad_gate.shape[1]
    sent_gate_up = pair_send(normed_two, [grad_gate[:rows], grad_up[:rows]], reduce_a[0], back_other)
    sent_down = pair_send(cot, [hidden_all[:rows]], reduce_b[0], back_other)
    sums_down = scatter_sum(pair_grad(sent_down, hidden_wide), reduce_b[0])
    sums_gate_up = scatter_sum(pair_grad(sent_gate_up, 2 * hidden_wide), reduce_a[0])
    produced = jnp.concatenate(
        [slots(contract(after(x, grad_in_2), down_matrix, 1, 0)) for x in (hidden_1, hidden_2)], axis=1
    )
    grad_routed = contract(place_own, back_own, 0, 0) + partner(
        contract(place_other, back_other, 0, 0).astype(BF)
    ).astype(F32)

    def expert_sum(grad):
        total = my_part(grad, 0)
        for step in range(1, n_wt):
            w = lax.axis_index("wt")
            total = total + wt_to(part_of(grad, (w + step) % n_wt, 0).astype(BF), step).astype(F32)
        return total[None]

    grad_two = shared_back + grad_routed
    grad_part, grad_gain_mlp = rms_back(residual, gain_two, grad_two)
    grad_residual = cot.astype(F32) + grad_part
    grad_attn_own = grad_residual.astype(BF)
    grad_attn = wt_rows(grad_attn_own)
    grad_heads = wt_own_rows(contract(grad_attn, w_out, 1, 1).astype(BF))
    sent_out = pair_send(grad_attn_own, [heads_out], reduce_b[0], grad_heads)

    out_rows = swap_blocks(after(produced, grad_routed))

    grad_query, grad_query_latent, grad_keys = attend_back(
        query_cat, keys, seen, up_key, up_value, out_latent, log_total, grad_heads, cos, sin
    )
    grad_keys = after(grad_keys, out_rows)
    out_own, out_other = out_rows[:, :capacity].reshape(-1, D), out_rows[:, capacity:].reshape(-1, D)
    grad_keys_a, grad_keys_b = jnp.split(grad_keys, 2, axis=0)
    first_a, first_b = (ctx_unspread(x, o[-1:]) for x, o in ((grad_keys_a, order_a), (grad_keys_b, order_b)))
    steps = [lax.optimization_barrier((first_a, first_b))]
    for number in range(2, len(order_a) + 1):
        step = tuple(
            ctx_unspread(x, order[-number : 1 - number])
            for x, order in zip(steps[-1], (order_a, order_b))
        )
        steps.append(lax.optimization_barrier(step))
    sent_query = [
        pair_send(grad_query, [one_own[:, part * (D // 2) : (part + 1) * (D // 2)]], order[0], *steps[1])
        for part, order in ((0, reduce_a), (1, reduce_b))
    ]
    grad_keys = jnp.concatenate(steps[-1], axis=0)
    routed = (
        contract(high_own, out_own, 0, 0)
        + contract(low_own, out_own, 0, 0)
        + partner(
            (contract(high_other, out_other, 0, 0) + contract(low_other, out_other, 0, 0)).astype(BF)
        ).astype(F32)
    )
    mixed_out = (residual + shared_out + routed).astype(BF)
    def expert_sum(former, latter):
        former = after(jnp.concatenate(former, axis=0), grad_keys)
        latter = jnp.concatenate(latter, axis=0)
        w = lax.axis_index("wt")
        sums = [
            wt_to(contract(part_of(former, (w + way) % n_wt, 1), latter, 0, 0).astype(BF), way)
            for way in range(1, n_wt)
        ]
        total = contract(after(my_part(former, 1), *sums), latter, 0, 0)
        for got in sums:
            total = total + got.astype(F32)
        return total[None]

    rows_in = rows_own, rows_other
    grad_w_expert_gate = expert_sum(rows_in, (grad_gate_1, grad_gate_2))
    grad_w_expert_up = expert_sum(rows_in, (grad_up_1, grad_up_2))
    grad_w_expert_down = expert_sum((hidden_1, hidden_2), (grad_own, grad_other))

    grad_up_key = jnp.einsum(
        "thd,htr->hdr", query_nope, after(grad_query_latent, grad_keys), preferred_element_type=F32
    )
    grad_up_value = jnp.einsum(
        "thv,htr->hvr", after(grad_heads, grad_keys).reshape(rows, H, DV), out_latent.astype(BF), preferred_element_type=F32
    )
    up_grads = jnp.concatenate([grad_up_key, grad_up_value], axis=1).astype(BF)
    up_grads = up_grads.reshape(n_ctx, n_wt, -1, R)
    own_up = my_part(up_grads, 1).astype(F32)
    for step in range(1, n_wt):
        w = lax.axis_index("wt")
        own_up = own_up + wt_to(part_of(up_grads, (w + step) % n_wt, 1), step).astype(F32)
    sum_kv_up = Reduction(own_up.astype(BF).reshape(n_ctx, -1, R), reduce_a, after)

    query_all = wt_rows(grad_query)
    sums_out = scatter_sum(pair_grad(sent_out, heads_out.shape[1], grad_keys), reduce_b[0])
    sums_query = [
        Reduction(pair_grad(sent, D // 2, grad_keys), order[1:], after).send()
        for sent, order in zip(sent_query, (reduce_a, reduce_b))
    ]
    sum_kv_up.send(grad_keys)
    one_back = contract(query_all, w_query, 1, 1)

    grad_latent, grad_gain_kv = rms_back(latent_raw, gain_latent, grad_keys[:, :R])
    first, second = grad_keys[:, R : R + DR // 2], grad_keys[:, R + DR // 2 :]
    grad_kv = jnp.concatenate(
        [grad_latent, first * cos + second * sin, second * cos - first * sin], axis=1
    ).astype(BF)
    grad_kv_all = wt_rows(grad_kv)
    one_columns = my_part(one_all.reshape(-1, n_ctx, n_wt, D // (n_ctx * n_wt)), 2).reshape(-1, D // n_wt)
    kv_down_terms = contract(one_columns, grad_kv_all, 0, 0).astype(BF).reshape(n_ctx, -1, KW)
    kv_down_terms = lax.all_to_all(kv_down_terms, "ctx", 0, 0, tiled=True)
    grad_one = wt_own_rows(one_back + contract(grad_kv_all, w_kv_down, 1, 1))
    grad_inputs, grad_gain_attn = rms_back(inputs, gain_one, grad_one)
    grad_tokens = grad_residual + grad_inputs

    gain_grads = jnp.concatenate(
        [
            g.reshape(n_ctx, n_wt, -1)
            for g in (grad_gain_attn, grad_gain_mlp, grad_gain_kv)
        ],
        axis=2,
    )
    gain_grads = lax.all_to_all(gain_grads.reshape(n_ctx * n_wt, -1), ("ctx", "wt"), 0, 0, tiled=True)
    gain_total = after.seal(jnp.sum(gain_grads, axis=0))
    wide = D // (n_ctx * n_wt)
    grad_w_kv_down = jnp.sum(kv_down_terms.astype(F32), axis=0)
    grad_w_query = jnp.concatenate([part.result().T for part in sums_query], axis=0)
    grad_w_kv_up = sum_kv_up.result().T
    grad_w_shared_gate, grad_w_shared_up = jnp.split(sums_gate_up, 2, axis=1)
    grad_w_shared_down = sums_down.T
    grad_w_out = sums_out.T

    return (
        mixed_out[None],
        grad_tokens[None],
        gain_total[:wide],
        grad_w_query,
        grad_w_kv_down,
        gain_total[2 * wide :],
        grad_w_kv_up,
        grad_w_out,
        gain_total[wide : 2 * wide],
        grad_w_shared_gate,
        grad_w_shared_up,
        grad_w_shared_down,
        grad_w_expert_gate,
        grad_w_expert_up,
        grad_w_expert_down,
    )


def solution(mesh):
    placed = (
        P("wt", "ctx", None),
        P("wt"),
        P("wt", None),
        P("wt", None),
        P("wt"),
        P("wt", None),
        P("wt", None),
        P("wt"),
        P("wt", None),
        P("wt", None),
        P("wt", None),
        P("ctx", "wt", None),
        P("ctx", "wt", None),
        P("ctx", "wt", None),
        P(),
        P("wt", None),
        P("wt", "ctx", None),
        P("wt", "ctx", None),
        P("wt", "ctx", None),
    )
    return jax.shard_map(
        per_device,
        mesh=mesh,
        in_specs=placed,
        out_specs=(
            P("wt", "ctx", None),
            P("wt", "ctx", None),
            P(("ctx", "wt")),
            P(None, ("ctx", "wt")),
            P(("ctx", "wt"), None),
            P(("ctx", "wt")),
            P(None, ("ctx", "wt")),
            P(None, ("ctx", "wt")),
            P(("ctx", "wt")),
            P(("ctx", "wt"), None),
            P(("ctx", "wt"), None),
            P(None, ("ctx", "wt")),
            P("ctx", "wt", None),
            P("ctx", "wt", None),
            P("ctx", "wt", None),
        ),
        check_vma=False,
    )
```
